256 devices in a mesh: ctx: 32 (over x, z), tr: 2 (over core), tc: 4 (over y).
Axes of the slice: x: 4, y: 4, z: 8, core: 2. Of those that a mesh axis runs over, the one named last changes fastest.
Arguments:
- tokens: bfloat16 [8192, 4096], P('ctx'), may hold values from -6 to 6
- w_in: bfloat16 [4096, 10240], P(('ctx', 'tr'), 'tc'), may hold values from -0.09375 to 0.09375
- w_step: bfloat16 [4096, 128], P(('ctx', 'tr'), 'tc'), may hold values from -0.09375 to 0.09375
- conv_weight: float32 [4, 10240], P(None, 'tc'), may hold values from -3 to 3
- conv_bias: float32 [10240], P('tc'), may hold values from -3 to 3
- dt_bias: float32 [128], P('tc'), may hold values from -5 to -3
- decay_rate: float32 [128], P('tc'), may hold values from 0.0012207031 to 2
- turn_keep: float32 [128], P('tc'), may hold values from 0.6 to 0.85
- skip: float32 [128], P('tc'), may hold values from 0.5 to 2
- norm_gain: float32 [8192], P('tc'), may hold values from 0.5 to 1.5
- gate: bfloat16 [8192, 8192], P(('ctx', 'tr'), 'tc'), may hold values from -6 to 6
- segment_ids: int32 [8192], replicated, may hold values from 0 to 5, never falling along the last dimension, each value on 1 to 4096 neighbouring positions
- turn_start: int32 [8192], P(('ctx', 'tr')), may hold values 0 or 1
Outputs:
- normed: bfloat16 [8192, 8192], P(('ctx', 'tr'), 'tc')
The draws below stay inside these ranges and needn't reach their ends.
All inputs are finite; a program needn't handle non-finite values. No bound on the sum of `turn_start` on one device may be relied on, other than what follows from the above.
Results may differ from the reference program's by a relative error of at most 0.006.
Values may be sent and summed in bfloat16 or wider, within the bound.
A program may use at most 192 MiB of HBM per device.

```python
import math
import jax
import jax.numpy as jnp
import numpy as np
from jax import lax

D = 4096
GROUPS = 8
HEAD_GROUP = 16
HEAD_DIM = 64
STATE = 128
CONV = 4
SPAN = 128
HEADS = 128
INNER = 8192
CHANNELS = 10240
TOKENS = 8192


def draw_decay_rate(key, part):
    key = jax.random.fold_in(key, 11)
    pick_key, slow_key, fast_key = jax.random.split(key, 3)
    share = 0.5
    chosen = jax.random.uniform(pick_key, (HEADS,)) < share
    slow_rate = jnp.exp(jax.random.uniform(slow_key, (HEADS,), minval=jnp.log(10.0 / TOKENS), maxval=jnp.log(60.0 / TOKENS)))
    fast_rate = jnp.exp(jax.random.uniform(fast_key, (HEADS,), minval=jnp.log(0.3), maxval=jnp.log(2.0)))
    return jnp.where(chosen, slow_rate, fast_rate).astype(jnp.float32)


def draw_gate(key, part):
    key = jax.random.fold_in(key, 12)
    base_key, column_key = jax.random.split(key, 2)
    ramp = 3.0 ** (jnp.arange(INNER, dtype=jnp.float32) / INNER)
    column = ramp * jnp.exp(jax.random.uniform(column_key, (INNER,), minval=-0.4, maxval=0.4))
    base = jax.random.normal(base_key, (TOKENS, INNER))
    return jnp.clip(0.7 * base * column[None, :], -6.0, 6.0).astype(jnp.bfloat16)


def with_ends(result, rng, smallest, high):
    shape = result.shape
    index_at = [jax.random.randint(jax.random.fold_in(rng, axis), (), 0, shape[axis]) for axis in range(len(shape))]
    result = result.at[tuple(index_at)].set(smallest)
    longest = shape.index(max(shape))
    index_at[longest] = (index_at[longest] + 1) % shape[longest]
    return result.at[tuple(index_at)].set(high)


def steps_of(stream_key, extent, cuts, smallest, top_value):
    def one(dim, parts):
        steps = jax.random.uniform(jax.random.fold_in(jax.random.fold_in(stream_key, 6), dim), (parts,), jnp.float32, smallest / len(cuts), top_value / len(cuts))
        return jnp.repeat(jnp.exp(steps), extent[dim] // parts).reshape((-1,) + (1,) * (len(extent) - dim - 1))

    level = one(*cuts[0])
    for cut in cuts[1:]:
        level = level * one(*cut)
    return level


def length_profile(amount, total, reach, skew):
    portions = [(1 << 20) // math.isqrt(standing ** skew) + 1 for standing in range(2, amount + 1)]
    surplus, counts = total - reach - (amount - 1), [1] * (amount - 1)
    while surplus > 0:
        movable = [i for i in range(amount - 1) if counts[i] < reach]
        mass, remaining = sum([portions[i] for i in movable]), surplus
        for i in movable:
            extra = min(reach - counts[i], max(1, remaining * portions[i] // mass), surplus)
            counts[i] = counts[i] + extra
            surplus = surplus - extra
    return np.array([reach] + counts)


def uneven(key, amount, total, reach, lean):
    if amount == 2:
        one = jax.random.randint(key, (), max(1, total - reach), min(reach, total - 1) + 1)
        return jnp.stack([one, total - one])
    sizes = jnp.asarray(length_profile(amount, total, reach, lean), jnp.int32)
    pairs = (amount - 1) // 2
    giver, sink = sizes[1:1 + 2 * pairs:2], sizes[2:2 + 2 * pairs:2]
    slack = jnp.minimum(giver - 1, reach - sink)
    moved = jax.random.randint(jax.random.fold_in(key, 1), (pairs,), 0, 1 << 20) % (slack + 1)
    sizes = sizes.at[1:1 + 2 * pairs:2].set(giver - moved).at[2:2 + 2 * pairs:2].set(sink + moved)
    return sizes[jax.random.permutation(jax.random.fold_in(key, 2), amount)]


def bell_draw(key, extent, width, most, shards=(), kind=jnp.bfloat16):
    loudness = steps_of(key, extent, shards, -0.22, 0.18) if shards else 1.0
    values = jax.random.normal(key, extent, jnp.float32) * width * loudness
    return jnp.minimum(jnp.maximum(values, -most), most).astype(kind)


def setup_inputs(seed: int = 0) -> dict:
    key_list = jax.random.split(jax.random.key(seed), 14)
    return {
        "tokens": bell_draw(key_list[0], (TOKENS, D), 1.0, 6.0, ((0, 32),)),
        "w_in": bell_draw(key_list[1], (D, CHANNELS), D ** -0.5, 0.09375, ((0, 64), (1, 4))),
        "w_step": bell_draw(key_list[2], (D, HEADS), D ** -0.5, 0.09375, ((0, 64), (1, 4))),
        "conv_weight": bell_draw(key_list[3], (CONV, CHANNELS), CONV ** -0.5, 3.0, ((1, 4),), jnp.float32),
        "conv_bias": bell_draw(key_list[4], (CHANNELS,), 0.5, 3.0, ((0, 4),), jnp.float32),
        "dt_bias": jnp.clip(-5.0 + 2.0 * jax.random.uniform(key_list[5], (HEADS,), jnp.float32) ** steps_of(key_list[5], (HEADS,), ((0, 4),), -0.2, 0.2), -5.0, -3.0),
        "decay_rate": draw_decay_rate(jax.random.fold_in(key_list[13], 71), 0),
        "turn_keep": jnp.clip(0.6 + 0.25 * jax.random.uniform(key_list[7], (HEADS,), jnp.float32) ** steps_of(key_list[7], (HEADS,), ((0, 4),), -0.2, 0.2), 0.6, 0.85),
        "skip": jnp.clip(0.5 + 1.5 * jax.random.uniform(key_list[8], (HEADS,), jnp.float32) ** steps_of(key_list[8], (HEADS,), ((0, 4),), -0.2, 0.2), 0.5, 2.0),
        "norm_gain": jnp.clip(1.0 + 0.1 * jax.random.normal(key_list[9], (INNER,), jnp.float32), 0.5, 1.5),
        "gate": draw_gate(jax.random.fold_in(key_list[13], 71), 0),
        "segment_ids": jnp.searchsorted(jnp.cumsum(uneven(key_list[11], 6, TOKENS, TOKENS // 2, 0)), jnp.arange(TOKENS), side="right").astype(jnp.int32),
        "turn_start": with_ends((jax.random.randint(key_list[12], (TOKENS,), 0, TOKENS // 4) < 1).astype(jnp.int32), jax.random.fold_in(key_list[12], 1), 0, 1),
    }


EPSILON = 1e-05

def reference(tokens, w_in, w_step, conv_weight, conv_bias, dt_bias, decay_rate, turn_keep, skip, norm_gain, gate, segment_ids, turn_start):
    block_count = TOKENS // SPAN
    per_group = HEAD_GROUP * HEAD_DIM + 2 * STATE
    token_blocks = tokens.reshape(block_count, SPAN, D)
    gate_blocks = gate.reshape(block_count, SPAN, INNER)
    id_blocks = segment_ids.reshape(block_count, SPAN)
    turn_blocks = turn_start.reshape(block_count, SPAN)
    log_keep = jnp.log(turn_keep)
    positions = jnp.arange(SPAN)
    lower = positions[:, None] >= positions[None, :]

    def one_block(carry_in, block):
        carried, rim_rows, rim_ids = carry_in
        block_rows, gate_rows, seg_ids, turn_flags = block
        xbc = jnp.dot(block_rows, w_in, preferred_element_type=jnp.float32).astype(jnp.bfloat16)
        dt_raw = jnp.dot(block_rows, w_step, preferred_element_type=jnp.float32)
        extended = jnp.concatenate([rim_rows, xbc], axis=0)
        extended_ids = jnp.concatenate([rim_ids, seg_ids], axis=0)
        conv_sum = jnp.zeros(xbc.shape, jnp.float32) + conv_bias[None, :]
        for tap_index in range(CONV):
            tap_mask = (extended_ids[tap_index:tap_index + SPAN] == seg_ids).astype(jnp.float32)
            conv_sum = conv_sum + conv_weight[tap_index][None, :] * extended[tap_index:tap_index + SPAN].astype(jnp.float32) * tap_mask[:, None]
        mixed_rows = jax.nn.silu(conv_sum).astype(jnp.bfloat16)
        grouped = mixed_rows.reshape(SPAN, GROUPS, per_group)
        head_input = grouped[:, :, :HEAD_GROUP * HEAD_DIM].reshape(SPAN, HEADS, HEAD_DIM)
        b_matrix = grouped[:, :, HEAD_GROUP * HEAD_DIM:HEAD_GROUP * HEAD_DIM + STATE]
        c_matrix = grouped[:, :, HEAD_GROUP * HEAD_DIM + STATE:]
        step_size = jax.nn.softplus(dt_raw + dt_bias[None, :])
        log_decay = -decay_rate[None, :] * step_size + turn_flags.astype(jnp.float32)[:, None] * log_keep[None, :]
        cumulative = jnp.cumsum(log_decay, axis=0)
        prior_id = rim_ids[CONV - 2]
        allowed = (seg_ids[:, None] == seg_ids[None, :]) & lower
        cum_heads = cumulative.T
        log_gap = cum_heads[:, :, None] - cum_heads[:, None, :]
        decay_weight = jnp.exp(jnp.where(allowed[None, :, :], log_gap, -jnp.inf))
        scores = jnp.einsum('tgn,sgn->gts', c_matrix.astype(jnp.float32), b_matrix.astype(jnp.float32))
        scores = jnp.repeat(scores, HEAD_GROUP, axis=0)
        weights = (scores * decay_weight * step_size.T[:, None, :]).astype(jnp.bfloat16)
        output_diag = jnp.einsum('hts,shp->thp', weights.astype(jnp.float32), head_input.astype(jnp.float32))
        to_end = jnp.where((seg_ids == seg_ids[SPAN - 1])[:, None], jnp.exp(cumulative[SPAN - 1][None, :] - cumulative), 0.0)
        scaled = (head_input.astype(jnp.float32) * (to_end * step_size)[:, :, None]).astype(jnp.bfloat16)
        b_heads = jnp.repeat(b_matrix, HEAD_GROUP, axis=1)
        c_heads = jnp.repeat(c_matrix, HEAD_GROUP, axis=1)
        span_state = jnp.einsum('shp,shn->hpn', scaled.astype(jnp.float32), b_heads.astype(jnp.float32))
        span_decay = jnp.exp(cumulative[SPAN - 1]) * (seg_ids[SPAN - 1] == prior_id).astype(jnp.float32)
        from_start = jnp.where((seg_ids == prior_id)[:, None], jnp.exp(cumulative), 0.0)
        output_off = jnp.einsum('thn,hpn->thp', c_heads.astype(jnp.float32), carried, precision=lax.Precision.HIGHEST) * from_start[:, :, None]
        output_sum = output_diag + output_off + skip[None, :, None] * head_input.astype(jnp.float32)
        output_sum = output_sum.reshape(SPAN, INNER)
        gated_rows = output_sum * jax.nn.silu(gate_rows.astype(jnp.float32))
        mean_sq = lax.optimization_barrier(jnp.mean(gated_rows * gated_rows, axis=1))
        normed = (gated_rows * lax.rsqrt(mean_sq + EPSILON)[:, None] * norm_gain[None, :]).astype(jnp.bfloat16)
        carried_next = span_decay[:, None, None] * carried + span_state
        return ((carried_next, xbc[SPAN - (CONV - 1):], seg_ids[SPAN - (CONV - 1):]), normed)
    start_carry = (jnp.zeros((HEADS, HEAD_DIM, STATE), jnp.float32), jnp.zeros((CONV - 1, CHANNELS), jnp.bfloat16), jnp.full((CONV - 1,), -1, jnp.int32))
    finished, outputs = lax.scan(one_block, start_carry, (token_blocks, gate_blocks, id_blocks, turn_blocks))
    return outputs.reshape(TOKENS, INNER)
```

```python
import jax
import jax.numpy as jnp
from jax import lax
from jax.experimental import pallas as pl
from jax.experimental.pallas import tpu as pltpu
from jax.sharding import PartitionSpec as P

HEAD_GROUP = 16
HEAD_DIM = 64
STATE = 128
SPAN = 128
INNER = 8192
EPSILON = 1e-05

NX, NZ = 4, 8
ROWS = 256
SLAB = 1024
GROUP = 1280
WIDE = 1024
COLS = 256
CHUNKS = 5
RIM = 16
MESH = pl.DeviceIdType.MESH
F32, BF16 = jnp.float32, jnp.bfloat16
EXACT = lax.Precision.HIGHEST


def place():
    ctx = lax.axis_index("ctx")
    return lax.div(ctx, NZ), lax.rem(ctx, NZ), lax.axis_index("tr"), lax.axis_index("tc")


def turn(a, n):
    return lax.rem(a + n, n)


def remote(src, dst, send, recv, device):
    return pltpu.make_async_remote_copy(
        src_ref=src, dst_ref=dst, send_sem=send, recv_sem=recv, device_id=device, device_id_type=MESH
    )


def meet(devices):
    barrier = pltpu.get_barrier_semaphore()
    for device in devices:
        pl.semaphore_signal(barrier, inc=1, device_id=device, device_id_type=MESH)
    pl.semaphore_wait(barrier, len(devices))


def project_kernel(
    tokens, first, w_in, flags, xbc, dt, flags_out,
    toks, tok_relay, wg0, wg, part, rel_out, rel_in, nb_out, nb_in, dt_out, dt_in,
    s_local, s_tok, s_sib_s, s_sib_r, s_ring_s, s_ring_r, s_tok_s, s_tok_r, s_fwd_s, s_fwd_r,
    s_rel_s, s_rel_r, s_nb_s, s_nb_r, s_dt_s, s_dt_r, s_rim_s, s_rim_r, s_flag_s, s_flag_r,
):
    x, z, c, _ = place()
    ctx = lax.axis_index("ctx")
    at = lambda xx, zz: {"ctx": xx * NZ + zz}
    x_right, x_left, x_far = at(turn(x + 1, NX), z), at(turn(x + 3, NX), z), at(turn(x + 2, NX), z)
    z_right, z_left = at(x, turn(z + 1, NZ)), at(x, turn(z + 7, NZ))
    sibling = {"tr": 1 - c}
    after, before = {"ctx": turn(ctx + 1, NX * NZ)}, {"ctx": turn(ctx + NX * NZ - 1, NX * NZ)}

    local = []

    def fetch(src, dst):
        copy = pltpu.make_async_copy(src, dst, s_local.at[len(local)])
        copy.start()
        local.append(copy)

    def columns(group, j):
        return pl.ds(pl.multiple_of(group * GROUP + (j - 1) * COLS, 128), COLS)

    def slab(index):
        return pl.ds(pl.multiple_of(index * SLAB, 128), SLAB)

    fetch(first.at[c], wg0.at[z, c])
    for j in range(1, CHUNKS):
        fetch(w_in.at[:, columns(c, j)], wg.at[j - 1, z, c])
    own_tokens = pltpu.make_async_copy(tokens.at[:, slab(x)], toks.at[0], s_tok.at[0])
    own_flags = pltpu.make_async_copy(flags, flags_out.at[c], s_tok.at[1])
    own_tokens.start()
    own_flags.start()

    meet([x_right, x_left, x_far, x_far, z_right, z_left, sibling, after, before])

    started = []

    def send(copy):
        copy.start()
        started.append(copy)
        return copy

    from_sibling = [send(remote(first.at[1 - c], wg0.at[z, c], s_sib_s.at[0], s_sib_r.at[0], sibling))]
    for j in range(1, CHUNKS):
        from_sibling.append(
            send(remote(w_in.at[:, columns(1 - c, j)], wg.at[j - 1, z, c], s_sib_s.at[j], s_sib_r.at[j], sibling))
        )
    half = pl.multiple_of(c * 128, 128)
    relay_hop = [
        send(remote(tokens.at[pl.ds(half, 64), slab(turn(x + 2, NX))], tok_relay.at[0], s_tok_s.at[0], s_tok_r.at[0], x_right)),
        send(remote(tokens.at[pl.ds(half + 64, 64), slab(turn(x + 2, NX))], tok_relay.at[1], s_tok_s.at[1], s_tok_r.at[1], x_left)),
    ]
    near_hop = [
        send(remote(tokens.at[pl.ds(half, 128), slab(turn(x + 1, NX))], toks.at[3, pl.ds(half, 128)], s_tok_s.at[2], s_tok_r.at[2], x_right)),
        send(remote(tokens.at[pl.ds(half, 128), slab(turn(x + 3, NX))], toks.at[1, pl.ds(half, 128)], s_tok_s.at[3], s_tok_r.at[3], x_left)),
    ]
    flag_hop = send(remote(flags, flags_out.at[c], s_flag_s, s_flag_r, sibling))

    ring = {}

    def block(j, slot, piece=None):
        ref = wg0 if j == 0 else wg.at[j - 1]
        return ref.at[slot] if piece is None else ref.at[slot, piece]

    def ring_hop(j, h):
        if h == 0:
            local[j].wait()
            from_sibling[j].wait_recv()
        for way, sign, device in ((0, -1, z_right), (1, 1, z_left)):
            if h > 0:
                ring[way, h - 1, j].wait_recv()
            slot = turn(z + sign * h + NZ, NZ)
            piece = None if h < 3 else way
            ring[way, h, j] = send(
                remote(block(j, slot, piece), block(j, slot, piece), s_ring_s.at[way, h, j], s_ring_r.at[way, h, j], device)
            )

    relays, nears, rims, steps = {}, {}, {}, []

    def multiply(j):
        for way in range(2):
            ring[way, 3, j].wait_recv()
        if j == 0:
            w = wg0[:, :, :64, :].reshape(SLAB, COLS)
        else:
            w = wg[j - 1].reshape(SLAB, COLS)
        far = jnp.dot(toks[2], w, preferred_element_type=F32)
        rel_out[j, 0] = far[:128].astype(BF16)
        rel_out[j, 1] = far[128:].astype(BF16)
        for way, device in ((0, x_right), (1, x_left)):
            relays[way, j] = send(
                remote(rel_out.at[j, way], rel_in.at[j, way], s_rel_s.at[way, j], s_rel_r.at[way, j], device)
            )
        part[j, 1] = jnp.dot(toks[1], w, preferred_element_type=F32)
        part[j, 2] = jnp.dot(toks[3], w, preferred_element_type=F32)
        part[j, 0] = jnp.dot(toks[0], w, preferred_element_type=F32)

    def step_sums():
        heads = jnp.concatenate(
            [wg0[k, 0, 64:80, :128] + wg0[k, 1, 64:80, :128] for k in range(NZ)], axis=1
        )
        for d in (2, 1, 3, 0):
            sums = lax.dot_general(heads, toks[d], (((1,), (1,)), ((), ())), preferred_element_type=F32)
            if d == 0:
                dt[...] = sums
            else:
                dt_out[d - 1] = sums
                device = (x_right, x_far, x_left)[d - 1]
                steps.append(send(remote(dt_out.at[d - 1], dt_in.at[d - 1], s_dt_s.at[d - 1], s_dt_r.at[d - 1], device)))

    def pass_on(j):
        relays[0, j].wait_recv()
        nb_out[j, 0, :128] = (part[j, 1, :128] + rel_in[j, 0].astype(F32)).astype(BF16)
        nb_out[j, 0, 128:] = part[j, 1, 128:].astype(BF16)
        nears[0, j] = send(remote(nb_out.at[j, 0], nb_in.at[j, 0], s_nb_s.at[0, j], s_nb_r.at[0, j], x_right))
        relays[1, j].wait_recv()
        nb_out[j, 1, :128] = part[j, 2, :128].astype(BF16)
        nb_out[j, 1, 128:] = (part[j, 2, 128:] + rel_in[j, 1].astype(F32)).astype(BF16)
        nears[1, j] = send(remote(nb_out.at[j, 1], nb_in.at[j, 1], s_nb_s.at[1, j], s_nb_r.at[1, j], x_left))

    def finish(j):
        nears[0, j].wait_recv()
        nears[1, j].wait_recv()
        cols = pl.ds(WIDE if j == 0 else (j - 1) * COLS, COLS)
        xbc[RIM:, cols] = (part[j, 0] + (nb_in[j, 0].astype(F32) + nb_in[j, 1].astype(F32))).astype(BF16)
        rims[j] = send(remote(xbc.at[pl.ds(ROWS, RIM), cols], xbc.at[pl.ds(0, RIM), cols], s_rim_s.at[j], s_rim_r.at[j], after))

    relayed, forwards = [], []

    def relay_tokens():
        for way, device in ((0, x_right), (1, x_left)):
            relay_hop[way].wait_recv()
            rows = pl.ds(half + 64 * way, 64)
            relayed.append(send(remote(tok_relay.at[way], toks.at[2, rows], s_tok_s.at[4 + way], s_tok_r.at[4 + way], device)))

    def share_tokens():
        near_hop[0].wait_recv()
        near_hop[1].wait_recv()
        relayed[0].wait_recv()
        relayed[1].wait_recv()
        for d in (3, 1, 2):
            forwards.append(
                send(remote(toks.at[d, pl.ds(half, 128)], toks.at[d, pl.ds(half, 128)], s_fwd_s.at[d - 1], s_fwd_r.at[d - 1], sibling))
            )
        own_tokens.wait()
        for copy in forwards:
            copy.wait_recv()

    for tick in range(CHUNKS + 6):
        for h in (3, 2, 1, 0):
            if 0 <= tick - h < CHUNKS:
                ring_hop(tick - h, h)
        if tick == 1:
            relay_tokens()
        if tick == 4:
            share_tokens()
        if 0 <= tick - 4 < CHUNKS:
            multiply(tick - 4)
        if 0 <= tick - 5 < CHUNKS:
            pass_on(tick - 5)
        if tick == 4:
            step_sums()
        if 0 <= tick - 6 < CHUNKS:
            finish(tick - 6)
    for copy in steps:
        copy.wait_recv()
    dt[...] += dt_in[0] + dt_in[1] + dt_in[2]
    own_flags.wait()
    flag_hop.wait_recv()
    for j in range(CHUNKS):
        rims[j].wait_recv()
    for copy in started:
        copy.wait_send()


def project(tokens, first, w_in, flags):
    sem = pltpu.SemaphoreType.DMA
    return pl.pallas_call(
        project_kernel,
        out_shape=(
            jax.ShapeDtypeStruct((RIM + ROWS, GROUP), BF16),
            jax.ShapeDtypeStruct((HEAD_GROUP, ROWS), F32),
            jax.ShapeDtypeStruct((2, 8, 128), F32),
        ),
        in_specs=[pl.BlockSpec(memory_space=pl.ANY)] * 3 + [pl.BlockSpec(memory_space=pltpu.VMEM)],
        out_specs=[pl.BlockSpec(memory_space=pltpu.VMEM)] * 3,
        scratch_shapes=[
            pltpu.VMEM((NX, ROWS, SLAB), BF16),
            pltpu.VMEM((2, 64, SLAB), BF16),
            pltpu.VMEM((NZ, 2, 80, COLS), BF16),
            pltpu.VMEM((CHUNKS - 1, NZ, 2, 64, COLS), BF16),
            pltpu.VMEM((CHUNKS, 3, ROWS, COLS), F32),
            pltpu.VMEM((CHUNKS, 2, 128, COLS), BF16),
            pltpu.VMEM((CHUNKS, 2, 128, COLS), BF16),
            pltpu.VMEM((CHUNKS, 2, ROWS, COLS), BF16),
            pltpu.VMEM((CHUNKS, 2, ROWS, COLS), BF16),
            pltpu.VMEM((3, HEAD_GROUP, ROWS), F32),
            pltpu.VMEM((3, HEAD_GROUP, ROWS), F32),
            sem((CHUNKS,)),
            sem((2,)),
            sem((CHUNKS,)),
            sem((CHUNKS,)),
            sem((2, 4, CHUNKS)),
            sem((2, 4, CHUNKS)),
            sem((6,)),
            sem((6,)),
            sem((3,)),
            sem((3,)),
            sem((2, CHUNKS)),
            sem((2, CHUNKS)),
            sem((2, CHUNKS)),
            sem((2, CHUNKS)),
            sem((3,)),
            sem((3,)),
            sem((CHUNKS,)),
            sem((CHUNKS,)),
            sem,
            sem,
        ],
        compiler_params=pltpu.CompilerParams(
            collective_id=0, has_side_effects=True, vmem_limit_bytes=40 * 2**20
        ),
    )(tokens, first, w_in, flags)


def scan_kernel(
    xbc, dt, flags, gate, tok_col, tok_row, head_par, conv_par, chan_par, out,
    xs, osum, states, state_bf, columns, st_in, d_out, d_in, pre, tot_out, tot_in, e_out, e_in,
    back_out, back_in, gates, gated, gated_sib, sq_out, sq_in,
    s_gate, s_local, s_st_s, s_st_r, s_d_s, s_d_r, s_t_s, s_t_r, s_e_s, s_e_r, s_b_s, s_b_r, s_q_s, s_q_r, s_g_s, s_g_r, s_gate_r,
):
    x, z, c, y = place()
    z_peer = [None] + [{"ctx": x * NZ + turn(z + k, NZ)} for k in range(1, NZ)]
    x_peer = [None] + [{"ctx": turn(x + k, NX) * NZ + z} for k in range(1, NX)]
    row_peer = [
        {"tr": turn(c + a, 2), "tc": turn(y + b, 4)} for a in range(2) for b in range(4) if (a, b) != (0, 0)
    ]
    sibling = {"tr": 1 - c}
    own_cols = pl.ds(pl.multiple_of(c * WIDE, 128), WIDE)
    sib_cols = pl.ds(pl.multiple_of((1 - c) * WIDE, 128), WIDE)

    gate_local = pltpu.make_async_copy(gate.at[:, own_cols], gates.at[c], s_local)
    gate_local.start()
    meet(z_peer[1:] + x_peer[1:] + row_peer)
    started = []

    def send(copy):
        copy.start()
        started.append(copy)
        return copy

    gate_swap = send(remote(gate.at[:, sib_cols], gates.at[c], s_gate, s_gate_r, sibling))

    mine = head_par[pl.ds(pl.multiple_of(c * HEAD_GROUP, 8), HEAD_GROUP), :]
    step = jax.nn.softplus(dt[...] + mine[:, 0:1])
    turns = jnp.concatenate([flags[0, 0:1, :], flags[1, 0:1, :]], axis=1)
    log_decay = -mine[:, 1:2] * step + turns * mine[:, 2:3]
    row_at = lax.broadcasted_iota(jnp.int32, (SPAN, SPAN), 0)
    lane_at = lax.broadcasted_iota(jnp.int32, (SPAN, SPAN), 1)
    upper = (row_at <= lane_at).astype(F32)
    low_lanes = lane_at < HEAD_DIM
    spread_row = lax.broadcasted_iota(jnp.int32, (SPAN, WIDE), 0)
    spread_lane = lax.broadcasted_iota(jnp.int32, (SPAN, WIDE), 1)
    spread = (lax.shift_right_logical(spread_lane, 6) == spread_row - 32).astype(F32)

    cums, decays = [], []
    for b in range(2):
        span = slice(b * SPAN, (b + 1) * SPAN)
        cum = jnp.dot(log_decay[:, span], upper, precision=EXACT, preferred_element_type=F32)
        to_end = jnp.exp(cum[:, SPAN - 1 :] - cum) * step[:, span] * tok_row[2:3, span]
        from_start = jnp.exp(cum) * tok_row[1:2, span]
        rows = jnp.concatenate([cum, to_end, from_start, jnp.zeros((80, SPAN), F32)], axis=0)
        columns[b] = rows.T
        cums.append(cum)
        decays.append(jnp.dot(columns[b, 120:128], spread, precision=EXACT, preferred_element_type=F32)[7:8])

    def expand(b, first):
        return jnp.where(low_lanes, columns[b, :, first : first + 1], columns[b, :, first + 1 : first + 2])

    def conv(channel):
        cols = pl.ds(channel, 128)
        par = pl.ds(pl.multiple_of(c * GROUP + channel, 128), 128)
        ext = xbc[:, cols].astype(F32)
        total = conv_par[4:5, par] + jnp.zeros((ROWS, 128), F32)
        for k in range(3):
            total = total + conv_par[k : k + 1, par] * ext[RIM - 3 + k : RIM - 3 + k + ROWS] * tok_col[:, k : k + 1]
        total = total + conv_par[3:4, par] * ext[RIM:]
        return jax.nn.silu(total).astype(BF16)

    b_matrix, c_matrix = conv(WIDE), conv(WIDE + STATE)
    b_turned = [b_matrix[b * SPAN : (b + 1) * SPAN].T for b in range(2)]

    for pair in range(8):
        cols = slice(pair * 128, (pair + 1) * 128)
        heads = conv(pair * 128)
        xs[:, cols] = heads
        for b in range(2):
            scaled = (heads[b * SPAN : (b + 1) * SPAN].astype(F32) * expand(b, 16 + 2 * pair)).astype(BF16)
            states[b, :, cols] = jnp.dot(b_turned[b], scaled, preferred_element_type=F32)
        state_bf[:, :, cols] = (
            (decays[1][:, cols] * states[0, :, cols] + states[1, :, cols]).astype(BF16).reshape(NZ, 16, 128)
        )
    d_out[...] = columns[0, 120:128] * columns[1, 120:128]
    st_in[z] = state_bf[z]
    d_in[z] = d_out[...]
    st_hops, d_hops = [], []
    for k in range(1, NZ):
        d_hops.append(send(remote(d_out, d_in.at[z], s_d_s.at[k], s_d_r.at[k], z_peer[k])))
        st_hops.append(
            send(remote(state_bf.at[turn(z + k, NZ)], st_in.at[z], s_st_s.at[k], s_st_r.at[k], z_peer[k]))
        )

    for b in range(2):
        span = slice(b * SPAN, (b + 1) * SPAN)
        scores = lax.dot_general(
            c_matrix[span], b_matrix[span], (((1,), (1,)), ((), ())), preferred_element_type=F32
        )
        allowed = (tok_col[span, 3:4] == tok_row[0:1, span]) & (row_at >= lane_at)
        for pair in range(8):
            cols = slice(pair * 128, (pair + 1) * 128)
            halves = []
            for h in (2 * pair, 2 * pair + 1):
                gap = jnp.where(allowed, columns[b, :, h : h + 1] - cums[b][h : h + 1], -jnp.inf)
                halves.append((scores * jnp.exp(gap) * step[h : h + 1, span]).astype(BF16))
            heads = xs[span, cols]
            zero = jnp.zeros_like(heads)
            both = jnp.concatenate([jnp.where(low_lanes, heads, zero), jnp.where(low_lanes, zero, heads)], axis=0)
            diag = jnp.dot(jnp.concatenate(halves, axis=1), both, preferred_element_type=F32)
            skip = chan_par[0:1, pl.ds(pl.multiple_of(c * WIDE + pair * 128, 128), 128)]
            osum[span, cols] = diag + skip * heads.astype(F32)

    for hop in d_hops + st_hops:
        hop.wait_recv()
    per_chip = jnp.concatenate([d_in[k, 7:8] for k in range(NZ)], axis=0)
    wide = jnp.dot(per_chip, spread, precision=EXACT, preferred_element_type=F32)
    running, passed, ahead = jnp.zeros((16, WIDE), F32), jnp.ones((1, WIDE), F32), []
    row_decay = per_chip[0:1]
    for k in range(NZ):
        pre[k] = running
        ahead.append(passed)
        running = wide[k : k + 1] * running + st_in[k].astype(F32)
        passed = passed * wide[k : k + 1]
        if k:
            row_decay = row_decay * per_chip[k : k + 1]
    tot_out[...] = running.astype(BF16)
    e_out[...] = jnp.broadcast_to(row_decay, (8, 128))
    tot_in[x] = tot_out[...]
    e_in[x] = e_out[...]
    t_hops = []
    for k in range(1, NX):
        t_hops.append(send(remote(e_out, e_in.at[x], s_e_s.at[k], s_e_r.at[k], x_peer[k])))
        t_hops.append(send(remote(tot_out, tot_in.at[x], s_t_s.at[k], s_t_r.at[k], x_peer[k])))
    for hop in t_hops:
        hop.wait_recv()
    row_wide = jnp.dot(
        jnp.concatenate([e_in[k] for k in range(NX)], axis=0), spread, precision=EXACT, preferred_element_type=F32
    )
    entering = jnp.zeros((16, WIDE), F32)
    for k in range(NX):
        entering = jnp.where(k < x, row_wide[8 * k : 8 * k + 1] * entering + tot_in[k].astype(F32), entering)
    for k in range(NZ):
        back_out[k] = (pre[k] + ahead[k] * entering).astype(BF16)
    back_in[z] = back_out[z]
    b_hops = [
        send(remote(back_out.at[turn(z + k, NZ)], back_in.at[z], s_b_s.at[k], s_b_r.at[k], z_peer[k]))
        for k in range(1, NZ)
    ]
    gate_local.wait()
    gate_swap.wait_recv()
    for hop in b_hops:
        hop.wait_recv()

    squares = [jnp.zeros((SPAN, SPAN), F32)] * 2
    for pair in range(8):
        cols = slice(pair * 128, (pair + 1) * 128)
        carried = back_in[:, :, cols].reshape(STATE, 128)
        later = (decays[0][:, cols] * carried.astype(F32) + states[0, :, cols]).astype(BF16)
        for b, state in ((0, carried), (1, later)):
            span = slice(b * SPAN, (b + 1) * SPAN)
            off = jnp.dot(c_matrix[span], state, preferred_element_type=F32) * expand(b, 32 + 2 * pair)
            rows = (osum[span, cols] + off) * jax.nn.silu(gates[b, :, cols].astype(F32))
            gated[b, :, cols] = rows
            squares[b] = squares[b] + rows * rows
    swap = send(remote(gated.at[1 - c], gated_sib, s_g_s, s_g_r, sibling))
    sums = [jnp.sum(s.T, axis=0, keepdims=True) for s in squares]
    sq_out[...] = jnp.concatenate(sums + [jnp.zeros((6, SPAN), F32)], axis=0)
    q_hops = [
        send(remote(sq_out, sq_in.at[k], s_q_s.at[k], s_q_r.at[k], device)) for k, device in enumerate(row_peer)
    ]
    for hop in q_hops:
        hop.wait_recv()
    total = sq_out[...]
    for k in range(7):
        total = total + sq_in[k]
    scale = lax.rsqrt(total / INNER + EPSILON)
    scale = jnp.where(c == 0, scale[0:1], scale[1:2])
    scale = jnp.broadcast_to(scale, (SPAN, SPAN)).T[:, 0:1]
    out[:, own_cols] = (gated[c] * scale * chan_par[1:2, own_cols]).astype(BF16)
    swap.wait_recv()
    out[:, sib_cols] = (gated_sib[...] * scale * chan_par[1:2, sib_cols]).astype(BF16)
    for copy in started:
        copy.wait_send()


def scan(*arrays):
    sem = pltpu.SemaphoreType.DMA
    vmem = pl.BlockSpec(memory_space=pltpu.VMEM)
    return pl.pallas_call(
        scan_kernel,
        out_shape=jax.ShapeDtypeStruct((SPAN, 2 * WIDE), BF16),
        in_specs=[vmem] * 3 + [pl.BlockSpec(memory_space=pl.ANY)] + [vmem] * 5,
        out_specs=vmem,
        scratch_shapes=[
            pltpu.VMEM((ROWS, WIDE), BF16),
            pltpu.VMEM((ROWS, WIDE), F32),
            pltpu.VMEM((2, STATE, WIDE), F32),
            pltpu.VMEM((NZ, 16, WIDE), BF16),
            pltpu.VMEM((2, SPAN, 128), F32),
            pltpu.VMEM((NZ, 16, WIDE), BF16),
            pltpu.VMEM((8, 128), F32),
            pltpu.VMEM((NZ, 8, 128), F32),
            pltpu.VMEM((NZ, 16, WIDE), F32),
            pltpu.VMEM((16, WIDE), BF16),
            pltpu.VMEM((NX, 16, WIDE), BF16),
            pltpu.VMEM((8, 128), F32),
            pltpu.VMEM((NX, 8, 128), F32),
            pltpu.VMEM((NZ, 16, WIDE), BF16),
            pltpu.VMEM((NZ, 16, WIDE), BF16),
            pltpu.VMEM((2, SPAN, WIDE), BF16),
            pltpu.VMEM((2, SPAN, WIDE), F32),
            pltpu.VMEM((SPAN, WIDE), F32),
            pltpu.VMEM((8, 128), F32),
            pltpu.VMEM((7, 8, 128), F32),
            sem,
            sem,
            sem((NZ,)),
            sem((NZ,)),
            sem((NZ,)),
            sem((NZ,)),
            sem((NX,)),
            sem((NX,)),
            sem((NX,)),
            sem((NX,)),
            sem((NZ,)),
            sem((NZ,)),
            sem((7,)),
            sem((7,)),
            sem,
            sem,
            sem,
        ],
        compiler_params=pltpu.CompilerParams(
            collective_id=1, has_side_effects=True, vmem_limit_bytes=40 * 2**20
        ),
    )(*arrays)


def shards(
    tokens, w_in, w_step, conv_weight, conv_bias, dt_bias, decay_rate, turn_keep, skip, norm_gain, gate,
    segment_ids, turn_start,
):
    ctx, core = lax.axis_index("ctx"), lax.axis_index("tr")
    turned = w_step.T.reshape(2, HEAD_GROUP, 64)
    turned = jnp.where(core == 0, jnp.pad(turned, ((0, 0), (0, 0), (0, 192))), jnp.pad(turned, ((0, 0), (0, 0), (64, 128))))
    edges = jnp.stack([w_in[:, WIDE:GROUP], w_in[:, GROUP + WIDE :]])
    first = jnp.concatenate([edges, turned], axis=1)
    flags = jnp.broadcast_to(turn_start.astype(F32)[None, :], (8, SPAN))

    ids = lax.dynamic_slice_in_dim(
        jnp.concatenate([jnp.full((3,), -1, jnp.int32), segment_ids]), ctx * ROWS, ROWS + 3, 0
    )
    own = ids[3:]
    blocks = own.reshape(2, SPAN)
    prior = jnp.stack([ids[2], own[SPAN - 1]])
    tok_col = jnp.stack([(ids[k : k + ROWS] == own).astype(F32) for k in range(3)] + [own.astype(F32)], axis=1)
    tok_col = jnp.pad(tok_col, ((0, 0), (0, 124)))
    tok_row = jnp.stack(
        [
            own.astype(F32),
            (blocks == prior[:, None]).astype(F32).reshape(-1),
            (blocks == blocks[:, SPAN - 1 :]).astype(F32).reshape(-1),
        ]
    )
    tok_row = jnp.pad(tok_row, ((0, 5), (0, 0)))
    head_par = jnp.pad(jnp.stack([dt_bias, decay_rate, jnp.log(turn_keep)], axis=1), ((0, 0), (0, 125)))
    conv_par = jnp.concatenate([conv_weight, conv_bias[None], jnp.zeros((3, 2 * GROUP), F32)], axis=0)
    chan_par = jnp.concatenate(
        [jnp.repeat(skip, HEAD_DIM)[None], norm_gain[None], jnp.zeros((6, 2 * WIDE), F32)], axis=0
    )
    xbc, dt, both_flags = project(tokens, first, w_in, flags)
    return scan(xbc, dt, both_flags, gate, tok_col, tok_row, head_par, conv_par, chan_par)


def solution(mesh):
    in_specs = (
        P("ctx", None),
        P(("ctx", "tr"), "tc"),
        P(("ctx", "tr"), "tc"),
        P(None, "tc"),
        P("tc"),
        P("tc"),
        P("tc"),
        P("tc"),
        P("tc"),
        P("tc"),
        P(("ctx", "tr"), "tc"),
        P(),
        P(("ctx", "tr")),
    )
    out_specs = P(("ctx", "tr"), "tc")
    return jax.shard_map(shards, mesh=mesh, in_specs=in_specs, out_specs=out_specs, check_vma=False)
```

```python
import jax
import jax.numpy as jnp
from jax import lax
from jax.experimental import pallas as pl
from jax.experimental.pallas import tpu as pltpu
from jax.sharding import PartitionSpec as P

HEAD_GROUP = 16
HEAD_DIM = 64
STATE = 128
SPAN = 128
INNER = 8192
EPSILON = 1e-05

NX, NZ = 4, 8
ROWS = 256
SLAB = 1024
GROUP = 1280
WIDE = 1024
COLS = 256
CHUNKS = 5
RIM = 16
MESH = pl.DeviceIdType.MESH
F32, BF16 = jnp.float32, jnp.bfloat16
EXACT = lax.Precision.HIGHEST


def place():
    ctx = lax.axis_index("ctx")
    return lax.div(ctx, NZ), lax.rem(ctx, NZ), lax.axis_index("tr"), lax.axis_index("tc")


def turn(a, n):
    return lax.rem(a + n, n)


def remote(src, dst, send, recv, device):
    return pltpu.make_async_remote_copy(
        src_ref=src, dst_ref=dst, send_sem=send, recv_sem=recv, device_id=device, device_id_type=MESH
    )


def meet(devices):
    barrier = pltpu.get_barrier_semaphore()
    for device in devices:
        pl.semaphore_signal(barrier, inc=1, device_id=device, device_id_type=MESH)
    pl.semaphore_wait(barrier, len(devices))


ORDER = (
    "r02", "r01", "r00", "relay", "r12", "r11", "r10", "r22", "r20", "near", "r32", "r03", "far", "r30",
    "r21", "toks", "mul2", "r04", "mul0", "r31", "pass2", "r13", "r14", "mul1", "flags", "pass0", "r23",
    "r24", "pass1", "r33", "steps", "r34", "fin0", "fin2", "mul3", "mul4", "dt", "bc", "pass3", "fin1", "st2",
    "pass4", "fin3", "st1", "diag2", "diag1", "st3", "zs2", "fin4", "zs1", "st4", "xs2", "xs1", "zs3", "zs4",
    "xs3", "diag3", "xs4", "diag4", "out1", "out3", "out2", "out4",
)


def layer_kernel(
    tokens, w_in, w_step_hbm, conv_w_hbm, conv_b_hbm, dt_bias_hbm, rate_hbm, keep_hbm, skip_hbm, gain_hbm, gate, ids_hbm,
    turns_hbm, out, w_step, conv_w, conv_b, dt_bias, rate, keep, skip_row, par, gain, ids, turns,
    toks, tok_relay, wg0, wg, step_rows, part, rel_out, rel_in, nb_out, nb_in, dt_out, dt_in, dt_own, flags,
    xbc, id_col, masks, spread, head_col, columns, wide_row, bc, xs, osum, states, state_bf, st_in, d_out, d_in,
    wide_z, pre, tot_out, tot_in, e_out, e_in, wide_x, back_out, back_in, gates, gated, gated_sib, squares, sq_out, sq_in,
    s_small, s_local, s_own, s_sib_s, s_sib_r, s_ring_s, s_ring_r, s_tok_s, s_tok_r, s_fwd_s, s_fwd_r, s_rel_s, s_rel_r,
    s_nb_s, s_nb_r, s_dt_s, s_dt_r, s_rim_s, s_rim_r, s_flag_s, s_flag_r, s_gate_s, s_gate_r,
    s_st_s, s_st_r, s_d_s, s_d_r, s_t_s, s_t_r, s_e_s, s_e_r, s_b_s, s_b_r, s_q_s, s_q_r, s_g_s, s_g_r,
):
    x, z, c, y = place()
    ctx = lax.axis_index("ctx")
    at = lambda xx, zz: {"ctx": xx * NZ + zz}
    z_peer = [None] + [at(x, turn(z + k, NZ)) for k in range(1, NZ)]
    x_peer = [None] + [at(turn(x + k, NX), z) for k in range(1, NX)]
    row_peer = [
        {"tr": turn(c + a, 2), "tc": turn(y + b, 4)} for a in range(2) for b in range(4) if (a, b) != (0, 0)
    ]
    x_right, x_far, x_left = x_peer[1:]
    z_right, z_left = z_peer[1], z_peer[7]
    sibling = {"tr": 1 - c}
    after, before = {"ctx": turn(ctx + 1, NX * NZ)}, {"ctx": turn(ctx + NX * NZ - 1, NX * NZ)}

    def columns_of(group, j):
        start = WIDE if j == 0 else (j - 1) * COLS
        return pl.ds(pl.multiple_of(group * GROUP + start, 128), COLS)

    def slab(index):
        return pl.ds(pl.multiple_of(index * SLAB, 128), SLAB)

    def block(j, slot, piece=None):
        ref = wg0 if j == 0 else wg.at[j - 1]
        return ref.at[slot] if piece is None else ref.at[slot, piece]

    own_cols = pl.ds(pl.multiple_of(c * WIDE, 128), WIDE)
    sib_cols = pl.ds(pl.multiple_of((1 - c) * WIDE, 128), WIDE)

    small = []
    for k, (src, dst) in enumerate(
        (
            (w_step_hbm, w_step), (turns_hbm, turns), (ids_hbm, ids), (conv_w_hbm, conv_w), (conv_b_hbm, conv_b),
            (dt_bias_hbm, dt_bias), (rate_hbm, rate), (keep_hbm, keep), (skip_hbm, skip_row), (gain_hbm, gain),
        )
    ):
        small.append(pltpu.make_async_copy(src, dst, s_small.at[k]))
        small[-1].start()
    local = []
    for j in range(CHUNKS):
        target = wg0.at[z, c, pl.ds(0, 64)] if j == 0 else wg.at[j - 1, z, c]
        copy = pltpu.make_async_copy(w_in.at[:, columns_of(c, j)], target, s_local.at[j])
        copy.start()
        local.append(copy)
    own_tokens = pltpu.make_async_copy(tokens.at[:, slab(x)], toks.at[0], s_own.at[0])
    own_tokens.start()
    own_gate = pltpu.make_async_copy(gate.at[:, own_cols], gates.at[c], s_own.at[1])
    own_gate.start()

    small[0].wait()
    small[1].wait()
    weights = w_step[...].astype(F32)
    blank = jnp.zeros((2 * HEAD_GROUP, 64), F32)
    weights = jnp.where(
        c == 0, jnp.concatenate([weights, blank], axis=1), jnp.concatenate([blank, weights], axis=1)
    )
    for group in range(2):
        rows = weights[group * HEAD_GROUP : (group + 1) * HEAD_GROUP].astype(BF16)
        step_rows[group] = jnp.concatenate([rows, jnp.zeros((HEAD_GROUP, 128), BF16)], axis=1)
    wg0[z, c, 64:80, :] = step_rows[c]
    flags[c] = jnp.broadcast_to(turns[...].astype(F32), (8, SPAN))

    meet(z_peer[1:] + x_peer[1:] + row_peer + [after, before])

    started = []

    def send(src, dst, sems, index, device):
        if index is None:
            copy = remote(src, dst, sems[0], sems[1], device)
        else:
            copy = remote(src, dst, sems[0].at[index], sems[1].at[index], device)
        copy.start()
        started.append(copy)
        return copy

    sib = (s_sib_s, s_sib_r)
    from_sibling = [
        [
            send(w_in.at[:, columns_of(1 - c, 0)], wg0.at[z, c, pl.ds(0, 64)], sib, 0, sibling),
            send(step_rows.at[1 - c], wg0.at[z, c, pl.ds(64, 16)], sib, 5, sibling),
        ]
    ]
    for j in (2, 1, 3, 4):
        from_sibling.append([send(w_in.at[:, columns_of(1 - c, j)], wg.at[j - 1, z, c], sib, j, sibling)])
    from_sibling = [from_sibling[0], from_sibling[2], from_sibling[1], from_sibling[3], from_sibling[4]]
    half = pl.multiple_of(c * 128, 128)
    tok = (s_tok_s, s_tok_r)
    far_slab, right_slab, left_slab = (slab(turn(x + k, NX)) for k in (2, 1, 3))
    relay_hop = [
        send(tokens.at[pl.ds(half + 64 * way, 64), far_slab], tok_relay.at[way], tok, way, device)
        for way, device in ((0, x_right), (1, x_left))
    ]
    near_hop = [
        send(tokens.at[pl.ds(half, 128), right_slab], toks.at[3, pl.ds(half, 128)], tok, 2, x_right),
        send(tokens.at[pl.ds(half, 128), left_slab], toks.at[1, pl.ds(half, 128)], tok, 3, x_left),
    ]
    hops = {}

    def ring_hop(h, j):
        if h == 0:
            local[j].wait()
            for copy in from_sibling[j]:
                copy.wait_recv()
        for way, sign, device in ((0, -1, z_right), (1, 1, z_left)):
            if h > 0:
                hops["r", way, h - 1, j].wait_recv()
            slot = turn(z + sign * h + NZ, NZ)
            piece = None if h < 3 else way
            ref = block(j, slot, piece)
            hops["r", way, h, j] = send(ref, ref, (s_ring_s, s_ring_r), (way, h, j), device)

    row_at = lax.broadcasted_iota(jnp.int32, (SPAN, SPAN), 0)
    lane_at = lax.broadcasted_iota(jnp.int32, (SPAN, SPAN), 1)
    low_lanes = lane_at < HEAD_DIM
    id_rows = []

    def do_flags(_):
        hops["flag"] = send(flags.at[c], flags.at[c], (s_flag_s, s_flag_r), None, sibling)
        hops["gate"] = send(gate.at[:, sib_cols], gates.at[c], (s_gate_s, s_gate_r), None, sibling)
        for copy in small[2:]:
            copy.wait()
        prior = ids[pl.ds(jnp.maximum(2 * ctx - 1, 0), 1), :].astype(F32)
        id_rows.append(jnp.where(ctx == 0, -1.0, prior))
        for b in range(2):
            id_rows.append(ids[pl.ds(2 * ctx + b, 1), :].astype(F32))
        for b in range(3):
            id_col[b * SPAN : (b + 1) * SPAN] = jnp.broadcast_to(id_rows[b], (SPAN, SPAN)).T
        for k in range(3):
            masks[k] = (id_col[SPAN - 3 + k : SPAN - 3 + k + ROWS] == id_col[SPAN:]).astype(F32)
        rows = [jnp.concatenate([v[...], jnp.zeros((1, 96), F32)], axis=1) for v in (dt_bias, rate, keep, skip_row)]
        par[...] = jnp.concatenate(rows + [jnp.zeros((4, 128), F32)], axis=0)
        spread_row = lax.broadcasted_iota(jnp.int32, (SPAN, WIDE), 0)
        spread_lane = lax.shift_right_logical(lax.broadcasted_iota(jnp.int32, (SPAN, WIDE), 1), 6)
        spread[...] = (spread_lane == spread_row - 32).astype(F32)
        pick = (spread_lane == spread_row - c * HEAD_GROUP).astype(F32)
        wide_row[2] = jnp.dot(par[...], pick, precision=EXACT, preferred_element_type=F32)
        head_col[...] = jnp.concatenate([par[...], jnp.zeros((120, 128), F32)], axis=0).T

    def do_relay(_):
        for way, device in ((0, x_right), (1, x_left)):
            relay_hop[way].wait_recv()
            rows = pl.ds(half + 64 * way, 64)
            hops["relay", way] = send(tok_relay.at[way], toks.at[2, rows], tok, 4 + way, device)

    def share(d, way=None):
        rows = pl.ds(half, 128) if way is None else pl.ds(half + 64 * way, 64)
        ref, index = toks.at[d, rows], d - 1 if way is None else 3 * way + 1
        hops["share", index] = send(ref, ref, (s_fwd_s, s_fwd_r), index, sibling)

    def do_near(_):
        near_hop[0].wait_recv()
        share(3)
        near_hop[1].wait_recv()
        share(1)

    def do_far(_):
        for way in range(2):
            hops["relay", way].wait_recv()
            share(2, way)

    def do_toks(_):
        own_tokens.wait()
        for index in (0, 1, 2, 4):
            hops["share", index].wait_recv()

    def do_mul(j):
        for way in range(2):
            hops["r", way, 3, j].wait_recv()
        w = (wg0[:, :, :64, :] if j == 0 else wg[j - 1]).reshape(SLAB, COLS)
        far = jnp.dot(toks[2], w, preferred_element_type=F32)
        rel_out[j, 0] = far[:128].astype(BF16)
        rel_out[j, 1] = far[128:].astype(BF16)
        for way, device in ((0, x_right), (1, x_left)):
            hops["rel", way, j] = send(rel_out.at[j, way], rel_in.at[j, way], (s_rel_s, s_rel_r), (way, j), device)
        part[j, 1] = jnp.dot(toks[1], w, preferred_element_type=F32)
        part[j, 2] = jnp.dot(toks[3], w, preferred_element_type=F32)
        part[j, 0] = jnp.dot(toks[0], w, preferred_element_type=F32)

    def do_steps(_):
        heads = jnp.concatenate(
            [wg0[k, 0, 64:80, :128] + wg0[k, 1, 64:80, :128] for k in range(NZ)], axis=1
        )
        for d in (2, 1, 3, 0):
            sums = lax.dot_general(heads, toks[d], (((1,), (1,)), ((), ())), preferred_element_type=F32)
            if d == 0:
                dt_own[...] = sums
            else:
                dt_out[d - 1] = sums
                hops["dt", d] = send(dt_out.at[d - 1], dt_in.at[d - 1], (s_dt_s, s_dt_r), d - 1, x_peer[d])

    def do_pass(j):
        hops["rel", 0, j].wait_recv()
        nb_out[j, 0, :128] = (part[j, 1, :128] + rel_in[j, 0].astype(F32)).astype(BF16)
        nb_out[j, 0, 128:] = part[j, 1, 128:].astype(BF16)
        hops["nb", 0, j] = send(nb_out.at[j, 0], nb_in.at[j, 0], (s_nb_s, s_nb_r), (0, j), x_right)
        hops["rel", 1, j].wait_recv()
        nb_out[j, 1, :128] = part[j, 2, :128].astype(BF16)
        nb_out[j, 1, 128:] = (part[j, 2, 128:] + rel_in[j, 1].astype(F32)).astype(BF16)
        hops["nb", 1, j] = send(nb_out.at[j, 1], nb_in.at[j, 1], (s_nb_s, s_nb_r), (1, j), x_left)

    def do_fin(j):
        hops["nb", 0, j].wait_recv()
        hops["nb", 1, j].wait_recv()
        xbc[j, RIM:] = (part[j, 0] + (nb_in[j, 0].astype(F32) + nb_in[j, 1].astype(F32))).astype(BF16)
        hops["rim", j] = send(
            xbc.at[j, pl.ds(ROWS, RIM)], xbc.at[j, pl.ds(0, RIM)], (s_rim_s, s_rim_r), j, after
        )

    cums, steps, entered, left = [], [], [], []

    def do_dt(_):
        for d in (1, 2, 3):
            hops["dt", d].wait_recv()
        hops["flag"].wait_recv()
        mine = head_col[pl.ds(pl.multiple_of(c * HEAD_GROUP, 8), HEAD_GROUP), :]
        step = jax.nn.softplus(dt_own[...] + dt_in[0] + dt_in[1] + dt_in[2] + mine[:, 0:1])
        turned = jnp.concatenate([flags[0, 0:1, :], flags[1, 0:1, :]], axis=1)
        log_decay = -mine[:, 1:2] * step + turned * jnp.log(mine[:, 2:3])
        upper = (row_at <= lane_at).astype(F32)
        for b in range(2):
            span = slice(b * SPAN, (b + 1) * SPAN)
            row, before_it = id_rows[b + 1], id_rows[b][:, SPAN - 1 :]
            cum = jnp.dot(log_decay[:, span], upper, precision=EXACT, preferred_element_type=F32)
            steps.append(step[:, span])
            cums.append(cum)
            to_end = jnp.where(row == row[:, SPAN - 1 :], jnp.exp(cum[:, SPAN - 1 :] - cum) * step[:, span], 0.0)
            from_start = jnp.where(row == before_it, jnp.exp(cum), 0.0)
            columns[b] = jnp.concatenate([cum, to_end, from_start, jnp.zeros((80, SPAN), F32)], axis=0).T
            wide_row[b] = jnp.dot(columns[b, 120:128], spread[...], precision=EXACT, preferred_element_type=F32)
        d_out[...] = columns[0, 120:128] * columns[1, 120:128]
        d_in[z] = d_out[...]
        for k in range(1, NZ):
            hops["d", k] = send(d_out, d_in.at[z], (s_d_s, s_d_r), k, z_peer[k])

    def expand(b, first):
        return jnp.where(low_lanes, columns[b, :, first : first + 1], columns[b, :, first + 1 : first + 2])

    def conv(j, part_of):
        lanes = slice(part_of * 128, (part_of + 1) * 128)
        start = (WIDE if j == 0 else (j - 1) * COLS) + part_of * 128
        at_channels = pl.ds(pl.multiple_of(c * GROUP + start, 128), 128)
        ext = xbc[j, :, lanes].astype(F32)
        total = conv_b[pl.ds(c * (GROUP // 128) + start // 128, 1), :] + jnp.zeros((ROWS, 128), F32)
        for k in range(3):
            total = total + conv_w[k : k + 1, at_channels] * ext[RIM - 3 + k : RIM - 3 + k + ROWS] * masks[k]
        total = total + conv_w[3:4, at_channels] * ext[RIM:]
        return jax.nn.silu(total).astype(BF16)

    def do_bc(_):
        hops["rim", 0].wait_recv()
        b_matrix = conv(0, 0)
        bc[1] = conv(0, 1)
        bc[0] = b_matrix
        for b in range(2):
            bc[2, b * SPAN : (b + 1) * SPAN] = b_matrix[b * SPAN : (b + 1) * SPAN].T

    def do_st(j):
        hops["rim", j].wait_recv()
        q = j - 1
        for pair in range(2):
            lanes = slice(pair * 128, (pair + 1) * 128)
            heads = conv(j, pair)
            xs[q, :, lanes] = heads
            for b in range(2):
                span = slice(b * SPAN, (b + 1) * SPAN)
                scaled = (heads[span].astype(F32) * expand(b, 16 + 4 * q + 2 * pair)).astype(BF16)
                states[q, b, :, lanes] = jnp.dot(bc[2, span], scaled, preferred_element_type=F32)
        decay = wide_row[1, 7:8, q * COLS : (q + 1) * COLS]
        state_bf[q] = (decay * states[q, 0] + states[q, 1]).astype(BF16).reshape(NZ, 16, COLS)
        st_in[q, z] = state_bf[q, z]
        for k in (4, 3, 5, 2, 6, 1, 7):
            hops["st", q, k] = send(
                state_bf.at[q, turn(z + k, NZ)], st_in.at[q, z], (s_st_s, s_st_r), (q, k), z_peer[k]
            )

    def do_diag(j):
        q = j - 1
        for b in range(2):
            span = slice(b * SPAN, (b + 1) * SPAN)
            scores = lax.dot_general(
                bc[1, span], bc[0, span], (((1,), (1,)), ((), ())), preferred_element_type=F32
            )
            allowed = (id_col[SPAN + b * SPAN : 2 * SPAN + b * SPAN] == id_rows[b + 1]) & (row_at >= lane_at)
            for pair in range(2):
                lanes = slice(pair * 128, (pair + 1) * 128)
                halves = []
                for h in (4 * q + 2 * pair, 4 * q + 2 * pair + 1):
                    gap = jnp.where(allowed, columns[b, :, h : h + 1] - cums[b][h : h + 1], -jnp.inf)
                    halves.append((scores * jnp.exp(gap) * steps[b][h : h + 1]).astype(BF16))
                heads = xs[q, span, lanes]
                zero = jnp.zeros_like(heads)
                both = jnp.concatenate([jnp.where(low_lanes, heads, zero), jnp.where(low_lanes, zero, heads)], axis=0)
                diag = jnp.dot(jnp.concatenate(halves, axis=1), both, preferred_element_type=F32)
                skip = wide_row[2, 3:4, q * COLS + pair * 128 : q * COLS + (pair + 1) * 128]
                osum[q, span, lanes] = diag + skip * heads.astype(F32)

    def do_zs(j):
        q = j - 1
        if ("e", 1) not in hops:
            for k in range(1, NZ):
                hops["d", k].wait_recv()
            per_chip = jnp.concatenate([d_in[k, 7:8] for k in range(NZ)], axis=0)
            wide_z[...] = jnp.dot(per_chip, spread[...], precision=EXACT, preferred_element_type=F32)
            row_decay = per_chip[0:1]
            for k in range(1, NZ):
                row_decay = row_decay * per_chip[k : k + 1]
            e_out[...] = jnp.broadcast_to(row_decay, (8, 128))
            e_in[x] = e_out[...]
            for k in range(1, NX):
                hops["e", k] = send(e_out, e_in.at[x], (s_e_s, s_e_r), k, x_peer[k])
        for k in range(1, NZ):
            hops["st", q, k].wait_recv()
        running = jnp.zeros((16, COLS), F32)
        for k in range(NZ):
            pre[q, k] = running
            running = wide_z[k : k + 1, q * COLS : (q + 1) * COLS] * running + st_in[q, k].astype(F32)
        tot_out[q] = running.astype(BF16)
        tot_in[q, x] = tot_out[q]
        for k in (2, 1, 3):
            hops["t", q, k] = send(tot_out.at[q], tot_in.at[q, x], (s_t_s, s_t_r), (q, k), x_peer[k])

    def do_xs(j):
        q = j - 1
        lanes = slice(q * COLS, (q + 1) * COLS)
        if not entered:
            entered.append(j)
            for k in range(1, NX):
                hops["e", k].wait_recv()
            wide_x[...] = jnp.dot(
                jnp.concatenate([e_in[k] for k in range(NX)], axis=0), spread[...], precision=EXACT,
                preferred_element_type=F32,
            )
        for k in range(1, NX):
            hops["t", q, k].wait_recv()
        entering = jnp.zeros((16, COLS), F32)
        for k in range(NX):
            entering = jnp.where(
                k < x, wide_x[8 * k : 8 * k + 1, lanes] * entering + tot_in[q, k].astype(F32), entering
            )
        for k in range(NZ):
            back_out[q, k] = (pre[q, k] + entering).astype(BF16)
            entering = entering * wide_z[k : k + 1, lanes]
        back_in[q, z] = back_out[q, z]
        for k in (4, 3, 5, 2, 6, 1, 7):
            hops["b", q, k] = send(
                back_out.at[q, turn(z + k, NZ)], back_in.at[q, z], (s_b_s, s_b_r), (q, k), z_peer[k]
            )

    def do_out(j):
        q = j - 1
        first = not left
        left.append(j)
        if first:
            own_gate.wait()
            hops["gate"].wait_recv()
        for k in range(1, NZ):
            hops["b", q, k].wait_recv()
        for pair in range(2):
            lanes = slice(pair * 128, (pair + 1) * 128)
            cols = slice(q * COLS + pair * 128, q * COLS + (pair + 1) * 128)
            carried = back_in[q, :, :, lanes].reshape(STATE, 128)
            later = (wide_row[0, 7:8, cols] * carried.astype(F32) + states[q, 0, :, lanes]).astype(BF16)
            for b, state in ((0, carried), (1, later)):
                span = slice(b * SPAN, (b + 1) * SPAN)
                off = jnp.dot(bc[1, span], state, preferred_element_type=F32) * expand(b, 32 + 4 * q + 2 * pair)
                rows = (osum[q, span, lanes] + off) * jax.nn.silu(gates[b, :, cols].astype(F32))
                gated[q, b, :, lanes] = rows
                squares[b] = rows * rows if first and pair == 0 else squares[b] + rows * rows
        hops["g", q] = send(gated.at[q, 1 - c], gated_sib.at[q], (s_g_s, s_g_r), q, sibling)

    act = {
        "flags": do_flags, "relay": do_relay, "near": do_near, "far": do_far, "toks": do_toks, "mul": do_mul, "steps": do_steps, "pass": do_pass,
        "fin": do_fin, "dt": do_dt, "bc": do_bc, "st": do_st, "diag": do_diag, "zs": do_zs, "xs": do_xs, "out": do_out,
    }
    for word in ORDER:
        if word[0] == "r" and word[1:].isdigit():
            ring_hop(int(word[1]), int(word[2]))
        elif word[-1].isdigit():
            act[word[:-1]](int(word[-1]))
        else:
            act[word](0)

    sums = [jnp.sum(squares[b].T, axis=0, keepdims=True) for b in range(2)]
    sq_out[...] = jnp.concatenate(sums + [jnp.zeros((6, SPAN), F32)], axis=0)
    q_hops = [
        send(sq_out, sq_in.at[k], (s_q_s, s_q_r), k, device) for k, device in enumerate(row_peer)
    ]
    for hop in q_hops:
        hop.wait_recv()
    total = sq_out[...]
    for k in range(7):
        total = total + sq_in[k]
    scale = lax.rsqrt(total / INNER + EPSILON)
    scale = jnp.where(c == 0, scale[0:1], scale[1:2])
    scale = jnp.broadcast_to(scale, (SPAN, SPAN)).T
    for q in range(4):
        hops["g", q].wait_recv()
        for pair in range(2):
            lanes = slice(pair * 128, (pair + 1) * 128)
            for group, rows in ((c, gated[q, c, :, lanes]), (1 - c, gated_sib[q, :, lanes])):
                cols = pl.ds(pl.multiple_of(group * WIDE + q * COLS + pair * 128, 128), 128)
                out[:, cols] = (rows * scale * gain[:, cols]).astype(BF16)
    for copy in started:
        copy.wait_send()


def layer(*arrays):
    sem = pltpu.SemaphoreType.DMA
    vmem, hbm = pl.BlockSpec(memory_space=pltpu.VMEM), pl.BlockSpec(memory_space=pltpu.HBM)

    def pair(*shape):
        return [sem(shape)] * 2 if shape else [sem] * 2

    return pl.pallas_call(
        layer_kernel,
        out_shape=jax.ShapeDtypeStruct((SPAN, 2 * WIDE), BF16),
        in_specs=[hbm] * 13,
        out_specs=vmem,
        scratch_shapes=[
            pltpu.VMEM((2 * HEAD_GROUP, 64), BF16),
            pltpu.VMEM((4, 2 * GROUP), F32),
            pltpu.VMEM((2 * GROUP // 128, 128), F32),
            pltpu.VMEM((1, 2 * HEAD_GROUP), F32),
            pltpu.VMEM((1, 2 * HEAD_GROUP), F32),
            pltpu.VMEM((1, 2 * HEAD_GROUP), F32),
            pltpu.VMEM((1, 2 * HEAD_GROUP), F32),
            pltpu.VMEM((8, 128), F32),
            pltpu.VMEM((1, 2 * WIDE), F32),
            pltpu.VMEM((64, SPAN), jnp.int32),
            pltpu.VMEM((1, SPAN), jnp.int32),
            pltpu.VMEM((NX, ROWS, SLAB), BF16),
            pltpu.VMEM((2, 64, SLAB), BF16),
            pltpu.VMEM((NZ, 2, 80, COLS), BF16),
            pltpu.VMEM((CHUNKS - 1, NZ, 2, 64, COLS), BF16),
            pltpu.VMEM((2, HEAD_GROUP, COLS), BF16),
            pltpu.VMEM((CHUNKS, 3, ROWS, COLS), F32),
            pltpu.VMEM((CHUNKS, 2, 128, COLS), BF16),
            pltpu.VMEM((CHUNKS, 2, 128, COLS), BF16),
            pltpu.VMEM((CHUNKS, 2, ROWS, COLS), BF16),
            pltpu.VMEM((CHUNKS, 2, ROWS, COLS), BF16),
            pltpu.VMEM((3, HEAD_GROUP, ROWS), F32),
            pltpu.VMEM((3, HEAD_GROUP, ROWS), F32),
            pltpu.VMEM((HEAD_GROUP, ROWS), F32),
            pltpu.VMEM((2, 8, SPAN), F32),
            pltpu.VMEM((CHUNKS, RIM + ROWS, COLS), BF16),
            pltpu.VMEM((3 * SPAN, SPAN), F32),
            pltpu.VMEM((3, ROWS, 128), F32),
            pltpu.VMEM((SPAN, WIDE), F32),
            pltpu.VMEM((128, 128), F32),
            pltpu.VMEM((2, SPAN, 128), F32),
            pltpu.VMEM((3, 8, WIDE), F32),
            pltpu.VMEM((3, ROWS, STATE), BF16),
            pltpu.VMEM((4, ROWS, COLS), BF16),
            pltpu.VMEM((4, ROWS, COLS), F32),
            pltpu.VMEM((4, 2, STATE, COLS), F32),
            pltpu.VMEM((4, NZ, 16, COLS), BF16),
            pltpu.VMEM((4, NZ, 16, COLS), BF16),
            pltpu.VMEM((8, 128), F32),
            pltpu.VMEM((NZ, 8, 128), F32),
            pltpu.VMEM((NZ, WIDE), F32),
            pltpu.VMEM((4, NZ, 16, COLS), F32),
            pltpu.VMEM((4, 16, COLS), BF16),
            pltpu.VMEM((4, NX, 16, COLS), BF16),
            pltpu.VMEM((8, 128), F32),
            pltpu.VMEM((NX, 8, 128), F32),
            pltpu.VMEM((8 * NX, WIDE), F32),
            pltpu.VMEM((4, NZ, 16, COLS), BF16),
            pltpu.VMEM((4, NZ, 16, COLS), BF16),
            pltpu.VMEM((2, SPAN, WIDE), BF16),
            pltpu.VMEM((4, 2, SPAN, COLS), F32),
            pltpu.VMEM((4, SPAN, COLS), F32),
            pltpu.VMEM((2, SPAN, 128), F32),
            pltpu.VMEM((8, 128), F32),
            pltpu.VMEM((7, 8, 128), F32),
            sem((10,)),
            sem((CHUNKS,)),
            sem((2,)),
            *pair(CHUNKS + 1),
            *pair(2, 4, CHUNKS),
            *pair(6),
            *pair(5),
            *pair(2, CHUNKS),
            *pair(2, CHUNKS),
            *pair(3),
            *pair(CHUNKS),
            *pair(),
            *pair(),
            *pair(4, NZ),
            *pair(NZ),
            *pair(4, NX),
            *pair(NX),
            *pair(4, NZ),
            *pair(7),
            *pair(4),
        ],
        compiler_params=pltpu.CompilerParams(
            collective_id=0, has_side_effects=True, vmem_limit_bytes=62 * 2**20
        ),
    )(*arrays)


def shards(
    tokens, w_in, w_step, conv_weight, conv_bias, dt_bias, decay_rate, turn_keep, skip, norm_gain, gate,
    segment_ids, turn_start,
):
    return layer(
        tokens, w_in, w_step.T, conv_weight, conv_bias.reshape(-1, 128), dt_bias[None], decay_rate[None],
        turn_keep[None], skip[None], norm_gain[None], gate, segment_ids.reshape(-1, SPAN), turn_start[None],
    )


def solution(mesh):
    in_specs = (
        P("ctx", None),
        P(("ctx", "tr"), "tc"),
        P(("ctx", "tr"), "tc"),
        P(None, "tc"),
        P("tc"),
        P("tc"),
        P("tc"),
        P("tc"),
        P("tc"),
        P("tc"),
        P(("ctx", "tr"), "tc"),
        P(),
        P(("ctx", "tr")),
    )
    out_specs = P(("ctx", "tr"), "tc")
    return jax.shard_map(shards, mesh=mesh, in_specs=in_specs, out_specs=out_specs, check_vma=False)
```

```python
import jax
import jax.numpy as jnp
from jax import lax
from jax.experimental import pallas as pl
from jax.experimental.pallas import tpu as pltpu
from jax.sharding import PartitionSpec as P

HEAD_GROUP = 16
HEAD_DIM = 64
STATE = 128
SPAN = 128
INNER = 8192
EPSILON = 1e-05

NX, NZ = 4, 8
ROWS = 256
SLAB = 1024
GROUP = 1280
WIDE = 1024
COLS = 256
CHUNKS = 5
RIM = 16
MESH = pl.DeviceIdType.MESH
F32, BF16 = jnp.float32, jnp.bfloat16
EXACT = lax.Precision.HIGHEST


def place():
    ctx = lax.axis_index("ctx")
    return lax.div(ctx, NZ), lax.rem(ctx, NZ), lax.axis_index("tr"), lax.axis_index("tc")


def turn(a, n):
    return lax.rem(a + n, n)


def remote(src, dst, send, recv, device):
    return pltpu.make_async_remote_copy(
        src_ref=src, dst_ref=dst, send_sem=send, recv_sem=recv, device_id=device, device_id_type=MESH
    )


def greet(devices):
    barrier = pltpu.get_barrier_semaphore()
    for device in devices:
        pl.semaphore_signal(barrier, inc=1, device_id=device, device_id_type=MESH)
    return len(devices)


ORDER = (
    "r02", "r01", "r00", "relay", "r12", "r11", "r10", "r22", "r20", "near", "r32", "r03", "far", "r30",
    "r21", "toks", "mul2", "r04", "mul0", "r31", "pass2", "r13", "r14", "mul1", "flags", "pass0", "r23",
    "r24", "pass1", "r33", "steps", "r34", "fin0", "fin2", "mul3", "mul4", "dt", "bc", "pass3", "fin1", "st2",
    "pass4", "drain", "fin3", "st1", "diag2", "diag1", "st3", "zs2", "fin4", "zs1", "st4", "xs2", "xs1", "zs3", "drain", "zs4",
    "xs3", "diag3", "xs4", "diag4", "out1", "out3", "out2", "out4",
)


def layer_kernel(
    tokens, w_in, w_step_hbm, conv_w_hbm, conv_b_hbm, dt_bias_hbm, rate_hbm, keep_hbm, skip_hbm, gain_hbm, gate, ids_hbm,
    turns_hbm, out, w_step, conv_w, conv_b, dt_bias, rate, keep, skip_row, par, gain, ids, turns,
    toks, tok_relay, wg0, wg, step_rows, part, rel_out, rel_in, nb_out, nb_in, dt_out, dt_in, dt_own, flags,
    xbc, id_col, masks, spread, head_col, columns, wide_row, bc, xs, osum, states, state_bf, st_in, d_out, d_in,
    wide_z, pre, tot_out, tot_in, e_out, e_in, wide_x, back_out, back_in, gates, gated, gated_sib, squares, sq_out, sq_in,
    s_small, s_local, s_own, s_sib_s, s_sib_r, s_ring_s, s_ring_r, s_tok_s, s_tok_r, s_fwd_s, s_fwd_r, s_rel_s, s_rel_r,
    s_nb_s, s_nb_r, s_dt_s, s_dt_r, s_rim_s, s_rim_r, s_flag_s, s_flag_r, s_gate_s, s_gate_r,
    s_st_s, s_st_r, s_d_s, s_d_r, s_t_s, s_t_r, s_e_s, s_e_r, s_b_s, s_b_r, s_q_s, s_q_r, s_g_s, s_g_r,
):
    x, z, c, y = place()
    ctx = lax.axis_index("ctx")
    at = lambda xx, zz: {"ctx": xx * NZ + zz}
    z_peer = [None] + [at(x, turn(z + k, NZ)) for k in range(1, NZ)]
    x_peer = [None] + [at(turn(x + k, NX), z) for k in range(1, NX)]
    row_peer = [
        {"tr": turn(c + a, 2), "tc": turn(y + b, 4)} for a in range(2) for b in range(4) if (a, b) != (0, 0)
    ]
    x_right, x_far, x_left = x_peer[1:]
    z_right, z_left = z_peer[1], z_peer[7]
    sibling = {"tr": 1 - c}
    after, before = {"ctx": turn(ctx + 1, NX * NZ)}, {"ctx": turn(ctx + NX * NZ - 1, NX * NZ)}

    z_cross = [{**z_right, "tr": 1 - c}, {**z_left, "tr": 1 - c}]
    greeted = greet(z_peer[1:] + x_peer[1:] + row_peer + [after, before] + z_cross)

    def columns_of(group, j):
        start = WIDE if j == 0 else (j - 1) * COLS
        return pl.ds(pl.multiple_of(group * GROUP + start, 128), COLS)

    def slab(index):
        return pl.ds(pl.multiple_of(index * SLAB, 128), SLAB)

    def block(j, slot, piece=None):
        ref = wg0 if j == 0 else wg.at[j - 1]
        return ref.at[slot] if piece is None else ref.at[slot, piece]

    own_cols = pl.ds(pl.multiple_of(c * WIDE, 128), WIDE)
    sib_cols = pl.ds(pl.multiple_of((1 - c) * WIDE, 128), WIDE)

    small = []
    for k, (src, dst) in enumerate(
        (
            (w_step_hbm, w_step), (turns_hbm, turns), (ids_hbm, ids), (conv_w_hbm, conv_w), (conv_b_hbm, conv_b),
            (dt_bias_hbm, dt_bias), (rate_hbm, rate), (keep_hbm, keep), (skip_hbm, skip_row), (gain_hbm, gain),
        )
    ):
        small.append(pltpu.make_async_copy(src, dst, s_small.at[k]))
        small[-1].start()
    local = []
    for j in range(CHUNKS):
        target = wg0.at[z, c, pl.ds(0, 64)] if j == 0 else wg.at[j - 1, z, c]
        copy = pltpu.make_async_copy(w_in.at[:, columns_of(c, j)], target, s_local.at[j])
        copy.start()
        local.append(copy)
    own_tokens = pltpu.make_async_copy(tokens.at[:, slab(x)], toks.at[0], s_own.at[0])
    own_tokens.start()
    own_gate = pltpu.make_async_copy(gate.at[:, own_cols], gates.at[c], s_own.at[1])
    own_gate.start()

    small[0].wait()
    small[1].wait()
    weights = w_step[...].astype(F32)
    blank = jnp.zeros((2 * HEAD_GROUP, 64), F32)
    weights = jnp.where(
        c == 0, jnp.concatenate([weights, blank], axis=1), jnp.concatenate([blank, weights], axis=1)
    )
    for group in range(2):
        rows = weights[group * HEAD_GROUP : (group + 1) * HEAD_GROUP].astype(BF16)
        step_rows[group] = jnp.concatenate([rows, jnp.zeros((HEAD_GROUP, 128), BF16)], axis=1)
    wg0[z, c, 64:80, :] = step_rows[c]
    flags[c] = jnp.broadcast_to(turns[...].astype(F32), (8, SPAN))

    pl.semaphore_wait(pltpu.get_barrier_semaphore(), greeted)

    started = []

    def send(src, dst, sems, index, device):
        if index is None:
            copy = remote(src, dst, sems[0], sems[1], device)
        else:
            copy = remote(src, dst, sems[0].at[index], sems[1].at[index], device)
        copy.start()
        started.append(copy)
        return copy

    def send_all(pieces, whole, sems):
        for src, dst, device in pieces:
            remote(src, dst, sems[0], sems[1], device).start()
        copy = remote(whole[0], whole[1], sems[0], sems[1], pieces[0][2])
        started.append(copy)
        return copy

    sib = (s_sib_s, s_sib_r)
    from_sibling = [
        [
            send(w_in.at[:, columns_of(1 - c, 0)], wg0.at[z, c, pl.ds(0, 64)], sib, 0, sibling),
            send(step_rows.at[1 - c], wg0.at[z, c, pl.ds(64, 16)], sib, 5, sibling),
        ]
    ]
    for j in (2, 1, 3, 4):
        from_sibling.append([send(w_in.at[:, columns_of(1 - c, j)], wg.at[j - 1, z, c], sib, j, sibling)])
    from_sibling = [from_sibling[0], from_sibling[2], from_sibling[1], from_sibling[3], from_sibling[4]]
    half = pl.multiple_of(c * 128, 128)
    tok = (s_tok_s, s_tok_r)
    far_slab, right_slab, left_slab = (slab(turn(x + k, NX)) for k in (2, 1, 3))
    relay_hop = [
        send(tokens.at[pl.ds(half + 64 * way, 64), far_slab], tok_relay.at[way], tok, way, device)
        for way, device in ((0, x_right), (1, x_left))
    ]
    near_hop = [
        send(tokens.at[pl.ds(half, 128), right_slab], toks.at[3, pl.ds(half, 128)], tok, 2, x_right),
        send(tokens.at[pl.ds(half, 128), left_slab], toks.at[1, pl.ds(half, 128)], tok, 3, x_left),
    ]
    hops = {}

    def ring_hop(h, j):
        sems = (s_ring_s, s_ring_r)
        if h == 0:
            local[j].wait()
        for way, sign, device in ((0, -1, z_right), (1, 1, z_left)):
            if h == 0:
                other = z_cross[way]
                target = wg0.at[z, c, pl.ds(0, 64)] if j == 0 else wg.at[j - 1, z, c]
                hops["r", way, 0, j] = send(block(j, z, c), block(j, z, c), sems, (way, 0, j), device)
                hops["rx", way, j] = [send(w_in.at[:, columns_of(1 - c, j)], target, sems, (way, 4, j), other)]
                if j == 0:
                    hops["rx", way, j].append(
                        send(step_rows.at[1 - c], wg0.at[z, c, pl.ds(64, 16)], sems, (way, 5, j), other)
                    )
                continue
            hops["r", way, h - 1, j].wait_recv()
            if h == 1:
                for copy in hops["rx", way, j]:
                    copy.wait_recv()
            slot = turn(z + sign * h + NZ, NZ)
            piece = None if h < 3 else way
            ref = block(j, slot, piece)
            hops["r", way, h, j] = send(ref, ref, sems, (way, h, j), device)

    def drain(keep):
        while len(started) > keep:
            started.pop(0).wait_send()

    row_at = lax.broadcasted_iota(jnp.int32, (SPAN, SPAN), 0)
    lane_at = lax.broadcasted_iota(jnp.int32, (SPAN, SPAN), 1)
    low_lanes = lane_at < HEAD_DIM
    id_rows = []

    def do_flags(_):
        hops["flag"] = send(flags.at[c], flags.at[c], (s_flag_s, s_flag_r), None, sibling)
        hops["gate"] = send(gate.at[:, sib_cols], gates.at[c], (s_gate_s, s_gate_r), None, sibling)
        for copy in small[2:]:
            copy.wait()
        prior = ids[pl.ds(jnp.maximum(2 * ctx - 1, 0), 1), :].astype(F32)
        id_rows.append(jnp.where(ctx == 0, -1.0, prior))
        for b in range(2):
            id_rows.append(ids[pl.ds(2 * ctx + b, 1), :].astype(F32))
        for b in range(3):
            id_col[b * SPAN : (b + 1) * SPAN] = jnp.broadcast_to(id_rows[b], (SPAN, SPAN)).T
        for k in range(3):
            masks[k] = (id_col[SPAN - 3 + k : SPAN - 3 + k + ROWS] == id_col[SPAN:]).astype(F32)
        rows = [jnp.concatenate([v[...], jnp.zeros((1, 96), F32)], axis=1) for v in (dt_bias, rate, keep, skip_row)]
        par[...] = jnp.concatenate(rows + [jnp.zeros((4, 128), F32)], axis=0)
        spread_row = lax.broadcasted_iota(jnp.int32, (SPAN, WIDE), 0)
        spread_lane = lax.shift_right_logical(lax.broadcasted_iota(jnp.int32, (SPAN, WIDE), 1), 6)
        spread[...] = (spread_lane == spread_row - 32).astype(F32)
        pick = (spread_lane == spread_row - c * HEAD_GROUP).astype(F32)
        wide_row[2] = jnp.dot(par[...], pick, precision=EXACT, preferred_element_type=F32)
        head_col[...] = jnp.concatenate([par[...], jnp.zeros((120, 128), F32)], axis=0).T

    def do_relay(_):
        for way, device in ((0, x_right), (1, x_left)):
            relay_hop[way].wait_recv()
            rows = pl.ds(half + 64 * way, 64)
            hops["relay", way] = send(tok_relay.at[way], toks.at[2, rows], tok, 4 + way, device)

    def share(d, way=None):
        rows = pl.ds(half, 128) if way is None else pl.ds(half + 64 * way, 64)
        ref, index = toks.at[d, rows], d - 1 if way is None else 3 * way + 1
        hops["share", index] = send(ref, ref, (s_fwd_s, s_fwd_r), index, sibling)

    def do_near(_):
        near_hop[0].wait_recv()
        share(3)
        near_hop[1].wait_recv()
        share(1)

    def do_far(_):
        for way in range(2):
            hops["relay", way].wait_recv()
            share(2, way)

    def do_toks(_):
        own_tokens.wait()
        for index in (0, 1, 2, 4):
            hops["share", index].wait_recv()

    def do_mul(j):
        for way in range(2):
            hops["r", way, 3, j].wait_recv()
        for copy in from_sibling[j]:
            copy.wait_recv()
        w = (wg0[:, :, :64, :] if j == 0 else wg[j - 1]).reshape(SLAB, COLS)
        far = jnp.dot(toks[2], w, preferred_element_type=F32)
        rel_out[j, 0] = far[:128].astype(BF16)
        rel_out[j, 1] = far[128:].astype(BF16)
        for way, device in ((0, x_right), (1, x_left)):
            hops["rel", way, j] = send(rel_out.at[j, way], rel_in.at[j, way], (s_rel_s, s_rel_r), (way, j), device)
        part[j, 1] = jnp.dot(toks[1], w, preferred_element_type=F32)
        part[j, 2] = jnp.dot(toks[3], w, preferred_element_type=F32)
        part[j, 0] = jnp.dot(toks[0], w, preferred_element_type=F32)

    def do_steps(_):
        heads = jnp.concatenate(
            [wg0[k, 0, 64:80, :128] + wg0[k, 1, 64:80, :128] for k in range(NZ)], axis=1
        )
        for d in (2, 1, 3, 0):
            sums = lax.dot_general(heads, toks[d], (((1,), (1,)), ((), ())), preferred_element_type=F32)
            if d == 0:
                dt_own[...] = sums
            else:
                dt_out[d - 1] = sums
                hops["dt", d] = send(dt_out.at[d - 1], dt_in.at[d - 1], (s_dt_s, s_dt_r), d - 1, x_peer[d])

    def do_pass(j):
        hops["rel", 0, j].wait_recv()
        nb_out[j, 0, :128] = (part[j, 1, :128] + rel_in[j, 0].astype(F32)).astype(BF16)
        nb_out[j, 0, 128:] = part[j, 1, 128:].astype(BF16)
        hops["nb", 0, j] = send(nb_out.at[j, 0], nb_in.at[j, 0], (s_nb_s, s_nb_r), (0, j), x_right)
        hops["rel", 1, j].wait_recv()
        nb_out[j, 1, :128] = part[j, 2, :128].astype(BF16)
        nb_out[j, 1, 128:] = (part[j, 2, 128:] + rel_in[j, 1].astype(F32)).astype(BF16)
        hops["nb", 1, j] = send(nb_out.at[j, 1], nb_in.at[j, 1], (s_nb_s, s_nb_r), (1, j), x_left)

    def do_fin(j):
        hops["nb", 0, j].wait_recv()
        hops["nb", 1, j].wait_recv()
        xbc[j, RIM:] = (part[j, 0] + (nb_in[j, 0].astype(F32) + nb_in[j, 1].astype(F32))).astype(BF16)
        hops["rim", j] = send(
            xbc.at[j, pl.ds(ROWS, RIM)], xbc.at[j, pl.ds(0, RIM)], (s_rim_s, s_rim_r), j, after
        )

    cums, steps, entered, left = [], [], [], []

    def do_dt(_):
        for d in (1, 2, 3):
            hops["dt", d].wait_recv()
        hops["flag"].wait_recv()
        mine = head_col[pl.ds(pl.multiple_of(c * HEAD_GROUP, 8), HEAD_GROUP), :]
        step = jax.nn.softplus(dt_own[...] + dt_in[0] + dt_in[1] + dt_in[2] + mine[:, 0:1])
        turned = jnp.concatenate([flags[0, 0:1, :], flags[1, 0:1, :]], axis=1)
        log_decay = -mine[:, 1:2] * step + turned * jnp.log(mine[:, 2:3])
        upper = (row_at <= lane_at).astype(F32)
        for b in range(2):
            span = slice(b * SPAN, (b + 1) * SPAN)
            row, before_it = id_rows[b + 1], id_rows[b][:, SPAN - 1 :]
            cum = jnp.dot(log_decay[:, span], upper, precision=EXACT, preferred_element_type=F32)
            steps.append(step[:, span])
            cums.append(cum)
            to_end = jnp.where(row == row[:, SPAN - 1 :], jnp.exp(cum[:, SPAN - 1 :] - cum) * step[:, span], 0.0)
            from_start = jnp.where(row == before_it, jnp.exp(cum), 0.0)
            columns[b] = jnp.concatenate([cum, to_end, from_start, jnp.zeros((80, SPAN), F32)], axis=0).T
            wide_row[b] = jnp.dot(columns[b, 120:128], spread[...], precision=EXACT, preferred_element_type=F32)
        d_out[...] = columns[0, 120:128] * columns[1, 120:128]
        d_in[z] = d_out[...]
        seven = d_in.at[pl.ds(0, 7)]
        hops["d"] = send_all([(d_out, d_in.at[z], z_peer[k]) for k in range(1, NZ)], (seven, seven), (s_d_s, s_d_r))

    def expand(b, first):
        return jnp.where(low_lanes, columns[b, :, first : first + 1], columns[b, :, first + 1 : first + 2])

    def conv(j, part_of):
        lanes = slice(part_of * 128, (part_of + 1) * 128)
        start = (WIDE if j == 0 else (j - 1) * COLS) + part_of * 128
        at_channels = pl.ds(pl.multiple_of(c * GROUP + start, 128), 128)
        ext = xbc[j, :, lanes].astype(F32)
        total = conv_b[pl.ds(c * (GROUP // 128) + start // 128, 1), :] + jnp.zeros((ROWS, 128), F32)
        for k in range(3):
            total = total + conv_w[k : k + 1, at_channels] * ext[RIM - 3 + k : RIM - 3 + k + ROWS] * masks[k]
        total = total + conv_w[3:4, at_channels] * ext[RIM:]
        return jax.nn.silu(total).astype(BF16)

    def do_bc(_):
        hops["rim", 0].wait_recv()
        b_matrix = conv(0, 0)
        bc[1] = conv(0, 1)
        bc[0] = b_matrix
        for b in range(2):
            bc[2, b * SPAN : (b + 1) * SPAN] = b_matrix[b * SPAN : (b + 1) * SPAN].T

    def do_st(j):
        hops["rim", j].wait_recv()
        q = j - 1
        for pair in range(2):
            lanes = slice(pair * 128, (pair + 1) * 128)
            heads = conv(j, pair)
            xs[q, :, lanes] = heads
            for b in range(2):
                span = slice(b * SPAN, (b + 1) * SPAN)
                scaled = (heads[span].astype(F32) * expand(b, 16 + 4 * q + 2 * pair)).astype(BF16)
                states[q, b, :, lanes] = jnp.dot(bc[2, span], scaled, preferred_element_type=F32)
        decay = wide_row[1, 7:8, q * COLS : (q + 1) * COLS]
        state_bf[q] = (decay * states[q, 0] + states[q, 1]).astype(BF16).reshape(NZ, 16, COLS)
        st_in[q, z] = state_bf[q, z]
        hops["st", q] = send_all(
            [(state_bf.at[q, turn(z + k, NZ)], st_in.at[q, z], z_peer[k]) for k in (4, 3, 5, 2, 6, 1, 7)],
            (state_bf.at[q, pl.ds(0, 7)], st_in.at[q, pl.ds(0, 7)]),
            (s_st_s.at[q], s_st_r.at[q]),
        )

    def do_diag(j):
        q = j - 1
        for b in range(2):
            span = slice(b * SPAN, (b + 1) * SPAN)
            scores = lax.dot_general(
                bc[1, span], bc[0, span], (((1,), (1,)), ((), ())), preferred_element_type=F32
            )
            allowed = (id_col[SPAN + b * SPAN : 2 * SPAN + b * SPAN] == id_rows[b + 1]) & (row_at >= lane_at)
            for pair in range(2):
                lanes = slice(pair * 128, (pair + 1) * 128)
                halves = []
                for h in (4 * q + 2 * pair, 4 * q + 2 * pair + 1):
                    gap = jnp.where(allowed, columns[b, :, h : h + 1] - cums[b][h : h + 1], -jnp.inf)
                    halves.append((scores * jnp.exp(gap) * steps[b][h : h + 1]).astype(BF16))
                heads = xs[q, span, lanes]
                zero = jnp.zeros_like(heads)
                both = jnp.concatenate([jnp.where(low_lanes, heads, zero), jnp.where(low_lanes, zero, heads)], axis=0)
                diag = jnp.dot(jnp.concatenate(halves, axis=1), both, preferred_element_type=F32)
                skip = wide_row[2, 3:4, q * COLS + pair * 128 : q * COLS + (pair + 1) * 128]
                osum[q, span, lanes] = diag + skip * heads.astype(F32)

    def do_zs(j):
        q = j - 1
        if "e" not in hops:
            hops["d"].wait_recv()
            per_chip = jnp.concatenate([d_in[k, 7:8] for k in range(NZ)], axis=0)
            wide_z[...] = jnp.dot(per_chip, spread[...], precision=EXACT, preferred_element_type=F32)
            row_decay = per_chip[0:1]
            for k in range(1, NZ):
                row_decay = row_decay * per_chip[k : k + 1]
            e_out[...] = jnp.broadcast_to(row_decay, (8, 128))
            e_in[x] = e_out[...]
            three = e_in.at[pl.ds(0, 3)]
            hops["e"] = send_all([(e_out, e_in.at[x], x_peer[k]) for k in (2, 1, 3)], (three, three), (s_e_s, s_e_r))
        hops["st", q].wait_recv()
        running = jnp.zeros((16, COLS), F32)
        for k in range(NZ):
            pre[q, k] = running
            running = wide_z[k : k + 1, q * COLS : (q + 1) * COLS] * running + st_in[q, k].astype(F32)
        tot_out[q] = running.astype(BF16)
        tot_in[q, x] = tot_out[q]
        three = tot_in.at[q, pl.ds(0, 3)]
        hops["t", q] = send_all(
            [(tot_out.at[q], tot_in.at[q, x], x_peer[k]) for k in (2, 1, 3)], (three, three), (s_t_s.at[q], s_t_r.at[q])
        )

    def do_xs(j):
        q = j - 1
        lanes = slice(q * COLS, (q + 1) * COLS)
        if not entered:
            entered.append(j)
            hops["e"].wait_recv()
            wide_x[...] = jnp.dot(
                jnp.concatenate([e_in[k] for k in range(NX)], axis=0), spread[...], precision=EXACT,
                preferred_element_type=F32,
            )
        hops["t", q].wait_recv()
        entering = jnp.zeros((16, COLS), F32)
        for k in range(NX):
            entering = jnp.where(
                k < x, wide_x[8 * k : 8 * k + 1, lanes] * entering + tot_in[q, k].astype(F32), entering
            )
        for k in range(NZ):
            back_out[q, k] = (pre[q, k] + entering).astype(BF16)
            entering = entering * wide_z[k : k + 1, lanes]
        back_in[q, z] = back_out[q, z]
        hops["b", q] = send_all(
            [(back_out.at[q, turn(z + k, NZ)], back_in.at[q, z], z_peer[k]) for k in (4, 3, 5, 2, 6, 1, 7)],
            (back_out.at[q, pl.ds(0, 7)], back_in.at[q, pl.ds(0, 7)]),
            (s_b_s.at[q], s_b_r.at[q]),
        )

    def do_out(j):
        q = j - 1
        first = not left
        left.append(j)
        if first:
            own_gate.wait()
            hops["gate"].wait_recv()
        hops["b", q].wait_recv()
        for pair in range(2):
            lanes = slice(pair * 128, (pair + 1) * 128)
            cols = slice(q * COLS + pair * 128, q * COLS + (pair + 1) * 128)
            carried = back_in[q, :, :, lanes].reshape(STATE, 128)
            later = (wide_row[0, 7:8, cols] * carried.astype(F32) + states[q, 0, :, lanes]).astype(BF16)
            for b, state in ((0, carried), (1, later)):
                span = slice(b * SPAN, (b + 1) * SPAN)
                off = jnp.dot(bc[1, span], state, preferred_element_type=F32) * expand(b, 32 + 4 * q + 2 * pair)
                rows = (osum[q, span, lanes] + off) * jax.nn.silu(gates[b, :, cols].astype(F32))
                gated[q, b, :, lanes] = rows
                squares[b] = rows * rows if first and pair == 0 else squares[b] + rows * rows
        hops["g", q] = send(gated.at[q, 1 - c], gated_sib.at[q], (s_g_s, s_g_r), q, sibling)

    act = {
        "flags": do_flags, "relay": do_relay, "near": do_near, "far": do_far, "toks": do_toks, "mul": do_mul, "steps": do_steps, "pass": do_pass,
        "fin": do_fin, "dt": do_dt, "bc": do_bc, "st": do_st, "diag": do_diag, "drain": lambda _: drain(14), "zs": do_zs, "xs": do_xs, "out": do_out,
    }
    for word in ORDER:
        if word[0] == "r" and word[1:].isdigit():
            ring_hop(int(word[1]), int(word[2]))
        elif word[-1].isdigit():
            act[word[:-1]](int(word[-1]))
        else:
            act[word](0)

    sums = [jnp.sum(squares[b].T, axis=0, keepdims=True) for b in range(2)]
    sq_out[...] = jnp.concatenate(sums + [jnp.zeros((6, SPAN), F32)], axis=0)
    send_all(
        [(sq_out, sq_in.at[k], device) for k, device in enumerate(row_peer)], (sq_in, sq_in), (s_q_s, s_q_r)
    ).wait_recv()
    total = sq_out[...]
    for k in range(7):
        total = total + sq_in[k]
    scale = lax.rsqrt(total / INNER + EPSILON)
    scale = jnp.where(c == 0, scale[0:1], scale[1:2])
    scale = jnp.broadcast_to(scale, (SPAN, SPAN)).T
    for q in range(4):
        hops["g", q].wait_recv()
        for pair in range(2):
            lanes = slice(pair * 128, (pair + 1) * 128)
            for group, rows in ((c, gated[q, c, :, lanes]), (1 - c, gated_sib[q, :, lanes])):
                cols = pl.ds(pl.multiple_of(group * WIDE + q * COLS + pair * 128, 128), 128)
                out[:, cols] = (rows * scale * gain[:, cols]).astype(BF16)
    drain(0)


def layer(*arrays):
    sem = pltpu.SemaphoreType.DMA
    vmem, hbm = pl.BlockSpec(memory_space=pltpu.VMEM), pl.BlockSpec(memory_space=pltpu.HBM)

    def pair(*shape):
        return [sem(shape)] * 2 if shape else [sem] * 2

    return pl.pallas_call(
        layer_kernel,
        out_shape=jax.ShapeDtypeStruct((SPAN, 2 * WIDE), BF16),
        in_specs=[hbm] * 13,
        out_specs=vmem,
        scratch_shapes=[
            pltpu.VMEM((2 * HEAD_GROUP, 64), BF16),
            pltpu.VMEM((4, 2 * GROUP), F32),
            pltpu.VMEM((2 * GROUP // 128, 128), F32),
            pltpu.VMEM((1, 2 * HEAD_GROUP), F32),
            pltpu.VMEM((1, 2 * HEAD_GROUP), F32),
            pltpu.VMEM((1, 2 * HEAD_GROUP), F32),
            pltpu.VMEM((1, 2 * HEAD_GROUP), F32),
            pltpu.VMEM((8, 128), F32),
            pltpu.VMEM((1, 2 * WIDE), F32),
            pltpu.VMEM((64, SPAN), jnp.int32),
            pltpu.VMEM((1, SPAN), jnp.int32),
            pltpu.VMEM((NX, ROWS, SLAB), BF16),
            pltpu.VMEM((2, 64, SLAB), BF16),
            pltpu.VMEM((NZ, 2, 80, COLS), BF16),
            pltpu.VMEM((CHUNKS - 1, NZ, 2, 64, COLS), BF16),
            pltpu.VMEM((2, HEAD_GROUP, COLS), BF16),
            pltpu.VMEM((CHUNKS, 3, ROWS, COLS), F32),
            pltpu.VMEM((CHUNKS, 2, 128, COLS), BF16),
            pltpu.VMEM((CHUNKS, 2, 128, COLS), BF16),
            pltpu.VMEM((CHUNKS, 2, ROWS, COLS), BF16),
            pltpu.VMEM((CHUNKS, 2, ROWS, COLS), BF16),
            pltpu.VMEM((3, HEAD_GROUP, ROWS), F32),
            pltpu.VMEM((3, HEAD_GROUP, ROWS), F32),
            pltpu.VMEM((HEAD_GROUP, ROWS), F32),
            pltpu.VMEM((2, 8, SPAN), F32),
            pltpu.VMEM((CHUNKS, RIM + ROWS, COLS), BF16),
            pltpu.VMEM((3 * SPAN, SPAN), F32),
            pltpu.VMEM((3, ROWS, 128), F32),
            pltpu.VMEM((SPAN, WIDE), F32),
            pltpu.VMEM((128, 128), F32),
            pltpu.VMEM((2, SPAN, 128), F32),
            pltpu.VMEM((3, 8, WIDE), F32),
            pltpu.VMEM((3, ROWS, STATE), BF16),
            pltpu.VMEM((4, ROWS, COLS), BF16),
            pltpu.VMEM((4, ROWS, COLS), F32),
            pltpu.VMEM((4, 2, STATE, COLS), F32),
            pltpu.VMEM((4, NZ, 16, COLS), BF16),
            pltpu.VMEM((4, NZ, 16, COLS), BF16),
            pltpu.VMEM((8, 128), F32),
            pltpu.VMEM((NZ, 8, 128), F32),
            pltpu.VMEM((NZ, WIDE), F32),
            pltpu.VMEM((4, NZ, 16, COLS), F32),
            pltpu.VMEM((4, 16, COLS), BF16),
            pltpu.VMEM((4, NX, 16, COLS), BF16),
            pltpu.VMEM((8, 128), F32),
            pltpu.VMEM((NX, 8, 128), F32),
            pltpu.VMEM((8 * NX, WIDE), F32),
            pltpu.VMEM((4, NZ, 16, COLS), BF16),
            pltpu.VMEM((4, NZ, 16, COLS), BF16),
            pltpu.VMEM((2, SPAN, WIDE), BF16),
            pltpu.VMEM((4, 2, SPAN, COLS), F32),
            pltpu.VMEM((4, SPAN, COLS), F32),
            pltpu.VMEM((2, SPAN, 128), F32),
            pltpu.VMEM((8, 128), F32),
            pltpu.VMEM((7, 8, 128), F32),
            sem((10,)),
            sem((CHUNKS,)),
            sem((2,)),
            *pair(CHUNKS + 1),
            *pair(2, 6, CHUNKS),
            *pair(6),
            *pair(5),
            *pair(2, CHUNKS),
            *pair(2, CHUNKS),
            *pair(3),
            *pair(CHUNKS),
            *pair(),
            *pair(),
            *pair(4),
            *pair(),
            *pair(4),
            *pair(),
            *pair(4),
            *pair(),
            *pair(4),
        ],
        compiler_params=pltpu.CompilerParams(
            collective_id=0, has_side_effects=True, vmem_limit_bytes=62 * 2**20
        ),
    )(*arrays)


def shards(
    tokens, w_in, w_step, conv_weight, conv_bias, dt_bias, decay_rate, turn_keep, skip, norm_gain, gate,
    segment_ids, turn_start,
):
    return layer(
        tokens, w_in, w_step.T, conv_weight, conv_bias.reshape(-1, 128), dt_bias[None], decay_rate[None],
        turn_keep[None], skip[None], norm_gain[None], gate, segment_ids.reshape(-1, SPAN), turn_start[None],
    )


def solution(mesh):
    in_specs = (
        P("ctx", None),
        P(("ctx", "tr"), "tc"),
        P(("ctx", "tr"), "tc"),
        P(None, "tc"),
        P("tc"),
        P("tc"),
        P("tc"),
        P("tc"),
        P("tc"),
        P("tc"),
        P(("ctx", "tr"), "tc"),
        P(),
        P(("ctx", "tr")),
    )
    out_specs = P(("ctx", "tr"), "tc")
    return jax.shard_map(shards, mesh=mesh, in_specs=in_specs, out_specs=out_specs, check_vma=False)
```

```python
import jax
import jax.numpy as jnp
from jax import lax
from jax.experimental import pallas as pl
from jax.experimental.pallas import tpu as pltpu
from jax.sharding import PartitionSpec as P

HEAD_GROUP = 16
HEAD_DIM = 64
STATE = 128
SPAN = 128
INNER = 8192
EPSILON = 1e-05

NX, NZ = 4, 8
ROWS = 256
SLAB = 1024
GROUP = 1280
WIDE = 1024
COLS = 256
CHUNKS = 5
LAST = 4
RIM = 16
MESH = pl.DeviceIdType.MESH
F32, BF16 = jnp.float32, jnp.bfloat16
EXACT = lax.Precision.HIGHEST


def place():
    ctx = lax.axis_index("ctx")
    return lax.div(ctx, NZ), lax.rem(ctx, NZ), lax.axis_index("tr"), lax.axis_index("tc")


def turn(a, n):
    return lax.rem(a + n, n)


def remote(src, dst, send, recv, device):
    return pltpu.make_async_remote_copy(
        src_ref=src, dst_ref=dst, send_sem=send, recv_sem=recv, device_id=device, device_id_type=MESH
    )


def greet(devices):
    barrier = pltpu.get_barrier_semaphore()
    for device in devices:
        pl.semaphore_signal(barrier, inc=1, device_id=device, device_id_type=MESH)
    return len(devices)


ORDER = (
    "r02", "r00", "r01", "flags", "r12", "r10", "relay", "r11", "r22", "r20", "near", "r21", "r30", "far",
    "r32", "r03", "toks", "r31", "mul0", "r04", "mul2", "steps", "r13", "mul1", "pass0", "r14", "r23",
    "pass2", "r24", "r33", "pass1", "dt", "fin0", "r34", "mul3", "fin2", "mul4", "bc", "pass3", "fin1",
    "pass4", "drain", "st2", "st1", "fin3", "edge", "zs2", "zs1", "fin4", "st3", "st4", "xs1", "xs2", "zs3",
    "drain", "zs4", "diag2", "diag1", "xs3", "out1", "diag4", "xs4", "out2", "diag3", "out3", "out4",
)


def layer_kernel(
    tokens, w_in, w_step_hbm, conv_w_hbm, conv_b_hbm, dt_bias_hbm, rate_hbm, keep_hbm, skip_hbm, gate, ids_hbm,
    turns_hbm, out, w_step, conv_w, conv_b, dt_bias, rate, keep, skip_row, par, ids, turns,
    toks, tok_relay, wg0, wg, step_rows, part, rel_out, rel_in, nb_out, nb_in, dt_out, dt_in, dt_own, flags,
    xbc, id_col, masks, spread, head_col, columns, wide_row, bc, xs, osum, states, state_bf, st_in, d_out, d_in,
    wide_z, pre, tot_out, tot_in, e_out, e_in, wide_x, back_out, back_in, gates, gated, gated_sib, squares, sq_out, sq_in,
    s_small, s_local, s_own, s_sib_s, s_sib_r, s_ring_s, s_ring_r, s_tok_s, s_tok_r, s_fwd_s, s_fwd_r, s_rel_s, s_rel_r,
    s_nb_s, s_nb_r, s_dt_s, s_dt_r, s_rim_s, s_rim_r, s_flag_s, s_flag_r, s_gate_s, s_gate_r,
    s_st_s, s_st_r, s_d_s, s_d_r, s_t_s, s_t_r, s_e_s, s_e_r, s_b_s, s_b_r, s_q_s, s_q_r, s_g_s, s_g_r,
):
    x, z, c, y = place()
    ctx = lax.axis_index("ctx")
    at = lambda xx, zz: {"ctx": xx * NZ + zz}
    z_peer = [None] + [at(x, turn(z + k, NZ)) for k in range(1, NZ)]
    x_peer = [None] + [at(turn(x + k, NX), z) for k in range(1, NX)]
    row_peer = [
        {"tr": turn(c + a, 2), "tc": turn(y + b, 4)} for a in range(2) for b in range(4) if (a, b) != (0, 0)
    ]
    x_right, x_far, x_left = x_peer[1:]
    z_right, z_left = z_peer[1], z_peer[7]
    sibling = {"tr": 1 - c}
    after, before = {"ctx": turn(ctx + 1, NX * NZ)}, {"ctx": turn(ctx + NX * NZ - 1, NX * NZ)}

    z_cross = [{**z_right, "tr": 1 - c}, {**z_left, "tr": 1 - c}]
    greeted = greet(z_peer[1:] + x_peer[1:] + row_peer + [after, before] + z_cross)

    def columns_of(group, j):
        start = WIDE if j == 0 else (j - 1) * COLS
        return pl.ds(pl.multiple_of(group * GROUP + start, 128), COLS)

    def slab(index):
        return pl.ds(pl.multiple_of(index * SLAB, 128), SLAB)

    def block(j, slot, piece=None):
        ref = wg0 if j == 0 else wg.at[j - 1]
        return ref.at[slot] if piece is None else ref.at[slot, piece]

    own_cols = pl.ds(pl.multiple_of(c * WIDE, 128), WIDE)
    sib_cols = pl.ds(pl.multiple_of((1 - c) * WIDE, 128), WIDE)

    small = []
    for k, (src, dst) in enumerate(
        (
            (w_step_hbm, w_step), (turns_hbm, turns), (ids_hbm, ids), (conv_w_hbm, conv_w), (conv_b_hbm, conv_b),
            (dt_bias_hbm, dt_bias), (rate_hbm, rate), (keep_hbm, keep), (skip_hbm, skip_row),
        )
    ):
        small.append(pltpu.make_async_copy(src, dst, s_small.at[k]))
        small[-1].start()
    local = []
    for j in range(CHUNKS):
        target = wg0.at[z, c, pl.ds(0, 64)] if j == 0 else wg.at[j - 1, z, c]
        copy = pltpu.make_async_copy(w_in.at[:, columns_of(c, j)], target, s_local.at[j])
        copy.start()
        local.append(copy)
    own_tokens = pltpu.make_async_copy(tokens.at[:, slab(x)], toks.at[0], s_own.at[0])
    own_tokens.start()
    own_gate = pltpu.make_async_copy(gate.at[:, own_cols], gates.at[c], s_own.at[1])
    own_gate.start()

    small[0].wait()
    small[1].wait()
    weights = w_step[...].astype(F32)
    blank = jnp.zeros((2 * HEAD_GROUP, 64), F32)
    weights = jnp.where(
        c == 0, jnp.concatenate([weights, blank], axis=1), jnp.concatenate([blank, weights], axis=1)
    )
    for group in range(2):
        rows = weights[group * HEAD_GROUP : (group + 1) * HEAD_GROUP].astype(BF16)
        step_rows[group] = jnp.concatenate([rows, jnp.zeros((HEAD_GROUP, 128), BF16)], axis=1)
    wg0[z, c, 64:80, :] = step_rows[c]
    flags[c] = jnp.broadcast_to(turns[...].astype(F32), (8, SPAN))

    pl.semaphore_wait(pltpu.get_barrier_semaphore(), greeted)

    started = []

    def send(src, dst, sems, index, device):
        if index is None:
            copy = remote(src, dst, sems[0], sems[1], device)
        else:
            copy = remote(src, dst, sems[0].at[index], sems[1].at[index], device)
        copy.start()
        started.append(copy)
        return copy

    def send_all(pieces, whole, sems):
        for src, dst, device in pieces:
            remote(src, dst, sems[0], sems[1], device).start()
        copy = remote(whole[0], whole[1], sems[0], sems[1], pieces[0][2])
        started.append(copy)
        return copy

    sib = (s_sib_s, s_sib_r)
    from_sibling = [
        [
            send(w_in.at[:, columns_of(1 - c, 0)], wg0.at[z, c, pl.ds(0, 64)], sib, 0, sibling),
            send(step_rows.at[1 - c], wg0.at[z, c, pl.ds(64, 16)], sib, 5, sibling),
        ]
    ]
    for j in (2, 1, 3, 4):
        from_sibling.append([send(w_in.at[:, columns_of(1 - c, j)], wg.at[j - 1, z, c], sib, j, sibling)])
    from_sibling = [from_sibling[0], from_sibling[2], from_sibling[1], from_sibling[3], from_sibling[4]]
    half = pl.multiple_of(c * 128, 128)
    tok = (s_tok_s, s_tok_r)
    far_slab, right_slab, left_slab = (slab(turn(x + k, NX)) for k in (2, 1, 3))
    relay_hop = [
        send(tokens.at[pl.ds(half + 64 * way, 64), far_slab], tok_relay.at[way], tok, way, device)
        for way, device in ((0, x_right), (1, x_left))
    ]
    near_hop = [
        send(tokens.at[pl.ds(half, 128), right_slab], toks.at[3, pl.ds(half, 128)], tok, 2, x_right),
        send(tokens.at[pl.ds(half, 128), left_slab], toks.at[1, pl.ds(half, 128)], tok, 3, x_left),
    ]
    hops = {}

    def ring_hop(h, j):
        sems = (s_ring_s, s_ring_r)
        if h == 0:
            local[j].wait()
        for way, sign, device in ((0, -1, z_right), (1, 1, z_left)):
            if h == 0:
                other = z_cross[way]
                target = wg0.at[z, c, pl.ds(0, 64)] if j == 0 else wg.at[j - 1, z, c]
                hops["r", way, 0, j] = send(block(j, z, c), block(j, z, c), sems, (way, 0, j), device)
                hops["rx", way, j] = [send(w_in.at[:, columns_of(1 - c, j)], target, sems, (way, 4, j), other)]
                if j == 0:
                    hops["rx", way, j].append(
                        send(step_rows.at[1 - c], wg0.at[z, c, pl.ds(64, 16)], sems, (way, 5, j), other)
                    )
                continue
            hops["r", way, h - 1, j].wait_recv()
            if h == 1:
                for copy in hops["rx", way, j]:
                    copy.wait_recv()
            slot = turn(z + sign * h + NZ, NZ)
            piece = None if h < 3 else way
            ref = block(j, slot, piece)
            hops["r", way, h, j] = send(ref, ref, sems, (way, h, j), device)

    def drain(keep):
        while len(started) > keep:
            started.pop(0).wait_send()

    row_at = lax.broadcasted_iota(jnp.int32, (SPAN, SPAN), 0)
    lane_at = lax.broadcasted_iota(jnp.int32, (SPAN, SPAN), 1)
    low_lanes = lane_at < HEAD_DIM
    id_rows = []

    def do_flags(_):
        hops["flag"] = send(flags.at[c], flags.at[c], (s_flag_s, s_flag_r), None, sibling)
        hops["gate"] = send(gate.at[:, sib_cols], gates.at[c], (s_gate_s, s_gate_r), None, sibling)
        for copy in small[2:]:
            copy.wait()
        prior = ids[pl.ds(jnp.maximum(2 * ctx - 1, 0), 1), :].astype(F32)
        id_rows.append(jnp.where(ctx == 0, -1.0, prior))
        for b in range(2):
            id_rows.append(ids[pl.ds(2 * ctx + b, 1), :].astype(F32))
        for b in range(3):
            id_col[b * SPAN : (b + 1) * SPAN] = jnp.broadcast_to(id_rows[b], (SPAN, SPAN)).T
        for k in range(3):
            masks[k] = (id_col[SPAN - 3 + k : SPAN - 3 + k + ROWS] == id_col[SPAN:]).astype(F32)
        rows = [jnp.concatenate([v[...], jnp.zeros((1, 96), F32)], axis=1) for v in (dt_bias, rate, keep, skip_row)]
        par[...] = jnp.concatenate(rows + [jnp.zeros((4, 128), F32)], axis=0)
        spread_row = lax.broadcasted_iota(jnp.int32, (SPAN, WIDE), 0)
        spread_lane = lax.shift_right_logical(lax.broadcasted_iota(jnp.int32, (SPAN, WIDE), 1), 6)
        spread[...] = (spread_lane == spread_row - 32).astype(F32)
        pick = (spread_lane == spread_row - c * HEAD_GROUP).astype(F32)
        wide_row[2] = jnp.dot(par[...], pick, precision=EXACT, preferred_element_type=F32)
        head_col[...] = jnp.concatenate([par[...], jnp.zeros((120, 128), F32)], axis=0).T

    def do_relay(_):
        for way, device in ((0, x_right), (1, x_left)):
            relay_hop[way].wait_recv()
            rows = pl.ds(half + 64 * way, 64)
            hops["relay", way] = send(tok_relay.at[way], toks.at[2, rows], tok, 4 + way, device)

    def share(d, way=None):
        rows = pl.ds(half, 128) if way is None else pl.ds(half + 64 * way, 64)
        ref, index = toks.at[d, rows], d - 1 if way is None else 3 * way + 1
        hops["share", index] = send(ref, ref, (s_fwd_s, s_fwd_r), index, sibling)

    def do_near(_):
        near_hop[0].wait_recv()
        share(3)
        near_hop[1].wait_recv()
        share(1)

    def do_far(_):
        for way in range(2):
            hops["relay", way].wait_recv()
            share(2, way)

    def do_toks(_):
        own_tokens.wait()
        for index in (0, 1, 2, 4):
            hops["share", index].wait_recv()

    def do_mul(j):
        for way in range(2):
            hops["r", way, 3, j].wait_recv()
        for copy in from_sibling[j]:
            copy.wait_recv()
        w = (wg0[:, :, :64, :] if j == 0 else wg[j - 1]).reshape(SLAB, COLS)
        far = jnp.dot(toks[2], w, preferred_element_type=F32)
        rel_out[j, 0] = far[:128].astype(BF16)
        rel_out[j, 1] = far[128:].astype(BF16)
        for way, device in ((0, x_right), (1, x_left)):
            hops["rel", way, j] = send(rel_out.at[j, way], rel_in.at[j, way], (s_rel_s, s_rel_r), (way, j), device)
        part[j, 1] = jnp.dot(toks[1], w, preferred_element_type=F32)
        part[j, 2] = jnp.dot(toks[3], w, preferred_element_type=F32)
        part[j, 0] = jnp.dot(toks[0], w, preferred_element_type=F32)

    def do_steps(_):
        heads = jnp.concatenate(
            [wg0[k, 0, 64:80, :128] + wg0[k, 1, 64:80, :128] for k in range(NZ)], axis=1
        )
        for d in (2, 1, 3, 0):
            sums = lax.dot_general(heads, toks[d], (((1,), (1,)), ((), ())), preferred_element_type=F32)
            if d == 0:
                dt_own[...] = sums
            else:
                dt_out[d - 1] = sums
                hops["dt", d] = send(dt_out.at[d - 1], dt_in.at[d - 1], (s_dt_s, s_dt_r), d - 1, x_peer[d])

    body = ROWS - RIM

    def send_sums(j, way, device):
        sems = (s_nb_s, s_nb_r)
        if j < LAST:
            hops["nb", way, j] = send(nb_out.at[j, way], nb_in.at[j, way], sems, (way, j), device)
            return
        rows = pl.ds(0, body)
        hops["nb", way, j] = send(nb_out.at[j, way, rows], nb_in.at[j, way, rows], sems, (way, j), device)

    def send_edge(way, device):
        rows = pl.ds(body, RIM)
        hops["edge", way] = send(
            nb_out.at[LAST, way, rows], nb_in.at[LAST, way, rows], (s_nb_s, s_nb_r), (way, CHUNKS), device
        )

    def do_pass(j):
        nb_out[j, 0, 128:] = part[j, 1, 128:].astype(BF16)
        nb_out[j, 1, :128] = part[j, 2, :128].astype(BF16)
        if j == LAST:
            send_edge(0, x_right)
        hops["rel", 0, j].wait_recv()
        nb_out[j, 0, :128] = (part[j, 1, :128] + rel_in[j, 0].astype(F32)).astype(BF16)
        if j < LAST:
            send_sums(j, 0, x_right)
        hops["rel", 1, j].wait_recv()
        nb_out[j, 1, 128:] = (part[j, 2, 128:] + rel_in[j, 1].astype(F32)).astype(BF16)
        if j == LAST:
            send_edge(1, x_left)
            send_sums(j, 0, x_right)
        send_sums(j, 1, x_left)

    def add_up(j, rows):
        return (part[j, 0, rows] + (nb_in[j, 0, rows].astype(F32) + nb_in[j, 1, rows].astype(F32))).astype(BF16)

    def send_rim(j):
        hops["rim", j] = send(
            xbc.at[j, pl.ds(ROWS, RIM)], xbc.at[j, pl.ds(0, RIM)], (s_rim_s, s_rim_r), j, after
        )

    def do_edge(_):
        hops["edge", 0].wait_recv()
        hops["edge", 1].wait_recv()
        xbc[LAST, ROWS:] = add_up(LAST, slice(body, ROWS))
        send_rim(LAST)

    def do_fin(j):
        hops["nb", 0, j].wait_recv()
        hops["nb", 1, j].wait_recv()
        if j == LAST:
            xbc[j, RIM:ROWS] = add_up(j, slice(0, body))
        else:
            xbc[j, RIM:] = add_up(j, slice(0, ROWS))
            send_rim(j)

    cums, steps, entered, left = [], [], [], []

    def do_dt(_):
        for d in (1, 2, 3):
            hops["dt", d].wait_recv()
        hops["flag"].wait_recv()
        mine = head_col[pl.ds(pl.multiple_of(c * HEAD_GROUP, 8), HEAD_GROUP), :]
        step = jax.nn.softplus(dt_own[...] + dt_in[0] + dt_in[1] + dt_in[2] + mine[:, 0:1])
        turned = jnp.concatenate([flags[0, 0:1, :], flags[1, 0:1, :]], axis=1)
        log_decay = -mine[:, 1:2] * step + turned * jnp.log(mine[:, 2:3])
        upper = (row_at <= lane_at).astype(F32)
        for b in range(2):
            span = slice(b * SPAN, (b + 1) * SPAN)
            row, before_it = id_rows[b + 1], id_rows[b][:, SPAN - 1 :]
            cum = jnp.dot(log_decay[:, span], upper, precision=EXACT, preferred_element_type=F32)
            steps.append(step[:, span])
            cums.append(cum)
            to_end = jnp.where(row == row[:, SPAN - 1 :], jnp.exp(cum[:, SPAN - 1 :] - cum) * step[:, span], 0.0)
            from_start = jnp.where(row == before_it, jnp.exp(cum), 0.0)
            columns[b] = jnp.concatenate([cum, to_end, from_start, jnp.zeros((80, SPAN), F32)], axis=0).T
            wide_row[b] = jnp.dot(columns[b, 120:128], spread[...], precision=EXACT, preferred_element_type=F32)
        d_out[...] = columns[0, 120:128] * columns[1, 120:128]
        d_in[z] = d_out[...]
        seven = d_in.at[pl.ds(0, 7)]
        hops["d"] = send_all([(d_out, d_in.at[z], z_peer[k]) for k in range(1, NZ)], (seven, seven), (s_d_s, s_d_r))

    def expand(b, first):
        return jnp.where(low_lanes, columns[b, :, first : first + 1], columns[b, :, first + 1 : first + 2])

    def conv(j, part_of):
        lanes = slice(part_of * 128, (part_of + 1) * 128)
        start = (WIDE if j == 0 else (j - 1) * COLS) + part_of * 128
        at_channels = pl.ds(pl.multiple_of(c * GROUP + start, 128), 128)
        ext = xbc[j, :, lanes].astype(F32)
        total = conv_b[pl.ds(c * (GROUP // 128) + start // 128, 1), :] + jnp.zeros((ROWS, 128), F32)
        for k in range(3):
            total = total + conv_w[k : k + 1, at_channels] * ext[RIM - 3 + k : RIM - 3 + k + ROWS] * masks[k]
        total = total + conv_w[3:4, at_channels] * ext[RIM:]
        return jax.nn.silu(total).astype(BF16)

    def do_bc(_):
        hops["rim", 0].wait_recv()
        b_matrix = conv(0, 0)
        bc[1] = conv(0, 1)
        bc[0] = b_matrix
        for b in range(2):
            bc[2, b * SPAN : (b + 1) * SPAN] = b_matrix[b * SPAN : (b + 1) * SPAN].T

    def do_st(j):
        hops["rim", j].wait_recv()
        q = j - 1
        for pair in range(2):
            lanes = slice(pair * 128, (pair + 1) * 128)
            heads = conv(j, pair)
            xs[q, :, lanes] = heads
            for b in range(2):
                span = slice(b * SPAN, (b + 1) * SPAN)
                scaled = (heads[span].astype(F32) * expand(b, 16 + 4 * q + 2 * pair)).astype(BF16)
                states[q, b, :, lanes] = jnp.dot(bc[2, span], scaled, preferred_element_type=F32)
        decay = wide_row[1, 7:8, q * COLS : (q + 1) * COLS]
        state_bf[q] = (decay * states[q, 0] + states[q, 1]).astype(BF16).reshape(NZ, 16, COLS)
        st_in[q, z] = state_bf[q, z]
        hops["st", q] = send_all(
            [(state_bf.at[q, turn(z + k, NZ)], st_in.at[q, z], z_peer[k]) for k in (4, 3, 5, 2, 6, 1, 7)],
            (state_bf.at[q, pl.ds(0, 7)], st_in.at[q, pl.ds(0, 7)]),
            (s_st_s.at[q], s_st_r.at[q]),
        )

    def do_diag(j):
        q = j - 1
        for b in range(2):
            span = slice(b * SPAN, (b + 1) * SPAN)
            scores = lax.dot_general(
                bc[1, span], bc[0, span], (((1,), (1,)), ((), ())), preferred_element_type=F32
            )
            allowed = (id_col[SPAN + b * SPAN : 2 * SPAN + b * SPAN] == id_rows[b + 1]) & (row_at >= lane_at)
            for pair in range(2):
                lanes = slice(pair * 128, (pair + 1) * 128)
                halves = []
                for h in (4 * q + 2 * pair, 4 * q + 2 * pair + 1):
                    gap = jnp.where(allowed, columns[b, :, h : h + 1] - cums[b][h : h + 1], -jnp.inf)
                    halves.append((scores * jnp.exp(gap) * steps[b][h : h + 1]).astype(BF16))
                heads = xs[q, span, lanes]
                zero = jnp.zeros_like(heads)
                both = jnp.concatenate([jnp.where(low_lanes, heads, zero), jnp.where(low_lanes, zero, heads)], axis=0)
                diag = jnp.dot(jnp.concatenate(halves, axis=1), both, preferred_element_type=F32)
                skip = wide_row[2, 3:4, q * COLS + pair * 128 : q * COLS + (pair + 1) * 128]
                osum[q, span, lanes] = diag + skip * heads.astype(F32)

    def do_zs(j):
        q = j - 1
        if "e" not in hops:
            hops["d"].wait_recv()
            per_chip = jnp.concatenate([d_in[k, 7:8] for k in range(NZ)], axis=0)
            wide_z[...] = jnp.dot(per_chip, spread[...], precision=EXACT, preferred_element_type=F32)
            row_decay = per_chip[0:1]
            for k in range(1, NZ):
                row_decay = row_decay * per_chip[k : k + 1]
            e_out[...] = jnp.broadcast_to(row_decay, (8, 128))
            e_in[x] = e_out[...]
            three = e_in.at[pl.ds(0, 3)]
            hops["e"] = send_all([(e_out, e_in.at[x], x_peer[k]) for k in (2, 1, 3)], (three, three), (s_e_s, s_e_r))
        hops["st", q].wait_recv()
        running = jnp.zeros((16, COLS), F32)
        for k in range(NZ):
            pre[q, k] = running
            running = wide_z[k : k + 1, q * COLS : (q + 1) * COLS] * running + st_in[q, k].astype(F32)
        tot_out[q] = running.astype(BF16)
        tot_in[q, x] = tot_out[q]
        three = tot_in.at[q, pl.ds(0, 3)]
        hops["t", q] = send_all(
            [(tot_out.at[q], tot_in.at[q, x], x_peer[k]) for k in (2, 1, 3)], (three, three), (s_t_s.at[q], s_t_r.at[q])
        )

    def do_xs(j):
        q = j - 1
        lanes = slice(q * COLS, (q + 1) * COLS)
        if not entered:
            entered.append(j)
            hops["e"].wait_recv()
            wide_x[...] = jnp.dot(
                jnp.concatenate([e_in[k] for k in range(NX)], axis=0), spread[...], precision=EXACT,
                preferred_element_type=F32,
            )
        hops["t", q].wait_recv()
        entering = jnp.zeros((16, COLS), F32)
        for k in range(NX):
            entering = jnp.where(
                k < x, wide_x[8 * k : 8 * k + 1, lanes] * entering + tot_in[q, k].astype(F32), entering
            )
        for k in range(NZ):
            back_out[q, k] = (pre[q, k] + entering).astype(BF16)
            entering = entering * wide_z[k : k + 1, lanes]
        back_in[q, z] = back_out[q, z]
        hops["b", q] = send_all(
            [(back_out.at[q, turn(z + k, NZ)], back_in.at[q, z], z_peer[k]) for k in (4, 3, 5, 2, 6, 1, 7)],
            (back_out.at[q, pl.ds(0, 7)], back_in.at[q, pl.ds(0, 7)]),
            (s_b_s.at[q], s_b_r.at[q]),
        )

    def do_out(j):
        q = j - 1
        first = not left
        left.append(j)
        if first:
            own_gate.wait()
            hops["gate"].wait_recv()
        hops["b", q].wait_recv()
        for pair in range(2):
            lanes = slice(pair * 128, (pair + 1) * 128)
            cols = slice(q * COLS + pair * 128, q * COLS + (pair + 1) * 128)
            carried = back_in[q, :, :, lanes].reshape(STATE, 128)
            later = (wide_row[0, 7:8, cols] * carried.astype(F32) + states[q, 0, :, lanes]).astype(BF16)
            for b, state in ((0, carried), (1, later)):
                span = slice(b * SPAN, (b + 1) * SPAN)
                off = jnp.dot(bc[1, span], state, preferred_element_type=F32) * expand(b, 32 + 4 * q + 2 * pair)
                rows = (osum[q, span, lanes] + off) * jax.nn.silu(gates[b, :, cols].astype(F32))
                gated[q, b, :, lanes] = rows
                squares[b] = rows * rows if first and pair == 0 else squares[b] + rows * rows
        hops["g", q] = send(gated.at[q, 1 - c], gated_sib.at[q], (s_g_s, s_g_r), q, sibling)

    act = {
        "flags": do_flags, "relay": do_relay, "near": do_near, "far": do_far, "toks": do_toks, "mul": do_mul, "steps": do_steps, "pass": do_pass,
        "fin": do_fin, "edge": do_edge, "dt": do_dt, "bc": do_bc, "st": do_st, "diag": do_diag, "drain": lambda _: drain(14), "zs": do_zs, "xs": do_xs, "out": do_out,
    }
    for word in ORDER:
        if word[0] == "r" and word[1:].isdigit():
            ring_hop(int(word[1]), int(word[2]))
        elif word[-1].isdigit():
            act[word[:-1]](int(word[-1]))
        else:
            act[word](0)

    sums = [jnp.sum(squares[b].T, axis=0, keepdims=True) for b in range(2)]
    sq_out[...] = jnp.concatenate(sums + [jnp.zeros((6, SPAN), F32)], axis=0)
    send_all(
        [(sq_out, sq_in.at[k], device) for k, device in enumerate(row_peer)], (sq_in, sq_in), (s_q_s, s_q_r)
    ).wait_recv()
    total = sq_out[...]
    for k in range(7):
        total = total + sq_in[k]
    scale = lax.rsqrt(total / INNER + EPSILON)
    scale = jnp.where(c == 0, scale[0:1], scale[1:2])
    scale = jnp.broadcast_to(scale, (SPAN, SPAN)).T
    for q in range(4):
        hops["g", q].wait_recv()
        for pair in range(2):
            lanes = slice(pair * 128, (pair + 1) * 128)
            for group, rows in ((c, gated[q, c, :, lanes]), (1 - c, gated_sib[q, :, lanes])):
                cols = pl.ds(pl.multiple_of(group * WIDE + q * COLS + pair * 128, 128), 128)
                out[:, cols] = rows * scale
    drain(0)


def layer(*arrays):
    sem = pltpu.SemaphoreType.DMA
    vmem, hbm = pl.BlockSpec(memory_space=pltpu.VMEM), pl.BlockSpec(memory_space=pltpu.HBM)

    def pair(*shape):
        return [sem(shape)] * 2 if shape else [sem] * 2

    return pl.pallas_call(
        layer_kernel,
        out_shape=jax.ShapeDtypeStruct((SPAN, 2 * WIDE), F32),
        in_specs=[hbm] * 12,
        out_specs=vmem,
        scratch_shapes=[
            pltpu.VMEM((2 * HEAD_GROUP, 64), BF16),
            pltpu.VMEM((4, 2 * GROUP), F32),
            pltpu.VMEM((2 * GROUP // 128, 128), F32),
            pltpu.VMEM((1, 2 * HEAD_GROUP), F32),
            pltpu.VMEM((1, 2 * HEAD_GROUP), F32),
            pltpu.VMEM((1, 2 * HEAD_GROUP), F32),
            pltpu.VMEM((1, 2 * HEAD_GROUP), F32),
            pltpu.VMEM((8, 128), F32),
            pltpu.VMEM((64, SPAN), jnp.int32),
            pltpu.VMEM((1, SPAN), jnp.int32),
            pltpu.VMEM((NX, ROWS, SLAB), BF16),
            pltpu.VMEM((2, 64, SLAB), BF16),
            pltpu.VMEM((NZ, 2, 80, COLS), BF16),
            pltpu.VMEM((CHUNKS - 1, NZ, 2, 64, COLS), BF16),
            pltpu.VMEM((2, HEAD_GROUP, COLS), BF16),
            pltpu.VMEM((CHUNKS, 3, ROWS, COLS), F32),
            pltpu.VMEM((CHUNKS, 2, 128, COLS), BF16),
            pltpu.VMEM((CHUNKS, 2, 128, COLS), BF16),
            pltpu.VMEM((CHUNKS, 2, ROWS, COLS), BF16),
            pltpu.VMEM((CHUNKS, 2, ROWS, COLS), BF16),
            pltpu.VMEM((3, HEAD_GROUP, ROWS), F32),
            pltpu.VMEM((3, HEAD_GROUP, ROWS), F32),
            pltpu.VMEM((HEAD_GROUP, ROWS), F32),
            pltpu.VMEM((2, 8, SPAN), F32),
            pltpu.VMEM((CHUNKS, RIM + ROWS, COLS), BF16),
            pltpu.VMEM((3 * SPAN, SPAN), F32),
            pltpu.VMEM((3, ROWS, 128), F32),
            pltpu.VMEM((SPAN, WIDE), F32),
            pltpu.VMEM((128, 128), F32),
            pltpu.VMEM((2, SPAN, 128), F32),
            pltpu.VMEM((3, 8, WIDE), F32),
            pltpu.VMEM((3, ROWS, STATE), BF16),
            pltpu.VMEM((4, ROWS, COLS), BF16),
            pltpu.VMEM((4, ROWS, COLS), F32),
            pltpu.VMEM((4, 2, STATE, COLS), F32),
            pltpu.VMEM((4, NZ, 16, COLS), BF16),
            pltpu.VMEM((4, NZ, 16, COLS), BF16),
            pltpu.VMEM((8, 128), F32),
            pltpu.VMEM((NZ, 8, 128), F32),
            pltpu.VMEM((NZ, WIDE), F32),
            pltpu.VMEM((4, NZ, 16, COLS), F32),
            pltpu.VMEM((4, 16, COLS), BF16),
            pltpu.VMEM((4, NX, 16, COLS), BF16),
            pltpu.VMEM((8, 128), F32),
            pltpu.VMEM((NX, 8, 128), F32),
            pltpu.VMEM((8 * NX, WIDE), F32),
            pltpu.VMEM((4, NZ, 16, COLS), BF16),
            pltpu.VMEM((4, NZ, 16, COLS), BF16),
            pltpu.VMEM((2, SPAN, WIDE), BF16),
            pltpu.VMEM((4, 2, SPAN, COLS), F32),
            pltpu.VMEM((4, SPAN, COLS), F32),
            pltpu.VMEM((2, SPAN, 128), F32),
            pltpu.VMEM((8, 128), F32),
            pltpu.VMEM((7, 8, 128), F32),
            sem((9,)),
            sem((CHUNKS,)),
            sem((2,)),
            *pair(CHUNKS + 1),
            *pair(2, 6, CHUNKS),
            *pair(6),
            *pair(5),
            *pair(2, CHUNKS),
            *pair(2, CHUNKS + 1),
            *pair(3),
            *pair(CHUNKS),
            *pair(),
            *pair(),
            *pair(4),
            *pair(),
            *pair(4),
            *pair(),
            *pair(4),
            *pair(),
            *pair(4),
        ],
        compiler_params=pltpu.CompilerParams(
            collective_id=0, has_side_effects=True, vmem_limit_bytes=62 * 2**20
        ),
    )(*arrays)


def shards(
    tokens, w_in, w_step, conv_weight, conv_bias, dt_bias, decay_rate, turn_keep, skip, norm_gain, gate,
    segment_ids, turn_start,
):
    rows = layer(
        tokens, w_in, w_step.T, conv_weight, conv_bias.reshape(-1, 128), dt_bias[None], decay_rate[None],
        turn_keep[None], skip[None], gate, segment_ids.reshape(-1, SPAN), turn_start[None],
    )
    return (rows * norm_gain[None, :]).astype(BF16)


def solution(mesh):
    in_specs = (
        P("ctx", None),
        P(("ctx", "tr"), "tc"),
        P(("ctx", "tr"), "tc"),
        P(None, "tc"),
        P("tc"),
        P("tc"),
        P("tc"),
        P("tc"),
        P("tc"),
        P("tc"),
        P(("ctx", "tr"), "tc"),
        P(),
        P(("ctx", "tr")),
    )
    out_specs = P(("ctx", "tr"), "tc")
    return jax.shard_map(shards, mesh=mesh, in_specs=in_specs, out_specs=out_specs, check_vma=False)
```

```python
import jax
import jax.numpy as jnp
from jax import lax
from jax.experimental import pallas as pl
from jax.experimental.pallas import tpu as pltpu
from jax.sharding import PartitionSpec as P

HEAD_GROUP = 16
HEAD_DIM = 64
STATE = 128
SPAN = 128
INNER = 8192
EPSILON = 1e-05

NX, NZ = 4, 8
ROWS = 256
SLAB = 1024
GROUP = 1280
WIDE = 1024
COLS = 256
CHUNKS = 5
LAST = 4
RIM = 16
MESH = pl.DeviceIdType.MESH
F32, BF16 = jnp.float32, jnp.bfloat16
EXACT = lax.Precision.HIGHEST


def place():
    ctx = lax.axis_index("ctx")
    return lax.div(ctx, NZ), lax.rem(ctx, NZ), lax.axis_index("tr"), lax.axis_index("tc")


def turn(a, n):
    return lax.rem(a + n, n)


def remote(src, dst, send, recv, device):
    return pltpu.make_async_remote_copy(
        src_ref=src, dst_ref=dst, send_sem=send, recv_sem=recv, device_id=device, device_id_type=MESH
    )


def greet(devices):
    barrier = pltpu.get_barrier_semaphore()
    for device in devices:
        pl.semaphore_signal(barrier, inc=1, device_id=device, device_id_type=MESH)
    return len(devices)


ORDER = (
    "r02", "r00", "r01", "flags", "r12", "r10", "relay", "r11", "r22", "r20", "near", "r21", "r30", "far",
    "r32", "r03", "toks", "r31", "mul0", "r04", "mul2", "steps", "r13", "mul1", "pass0", "r14", "r23",
    "pass2", "r24", "r33", "pass1", "dt", "fin0", "r34", "mul3", "fin2", "mul4", "bc", "pass3", "fin1",
    "pass4", "drain", "st2", "st1", "fin3", "edge", "zs2", "zs1", "st3", "fin4", "st4", "xs1", "xs2", "zs3",
    "drain", "zs4", "diag2", "diag1", "xs3", "out1", "diag4", "xs4", "out2", "diag3", "out3", "out4",
)


def layer_kernel(
    tokens, w_in, w_step_hbm, conv_w_hbm, conv_b_hbm, dt_bias_hbm, rate_hbm, keep_hbm, skip_hbm, gate, ids_hbm,
    turns_hbm, out, w_step, conv_w, conv_b, dt_bias, rate, keep, skip_row, par, ids, turns,
    toks, tok_relay, wg0, wg, step_rows, part, rel_out, rel_in, nb_out, nb_in, dt_out, dt_in, dt_own, flags,
    xbc, id_col, masks, spread, head_col, columns, wide_row, bc, xs, osum, states, state_bf, st_in, d_out, d_in,
    wide_z, pre, tot_out, tot_in, e_out, e_in, wide_x, back_out, back_in, gates, gated, gated_sib, squares, sq_out, sq_in,
    s_small, s_local, s_own, s_sib_s, s_sib_r, s_ring_s, s_ring_r, s_tok_s, s_tok_r, s_fwd_s, s_fwd_r, s_rel_s, s_rel_r,
    s_nb_s, s_nb_r, s_dt_s, s_dt_r, s_rim_s, s_rim_r, s_flag_s, s_flag_r, s_gate_s, s_gate_r,
    s_st_s, s_st_r, s_d_s, s_d_r, s_t_s, s_t_r, s_e_s, s_e_r, s_b_s, s_b_r, s_q_s, s_q_r, s_g_s, s_g_r,
):
    x, z, c, y = place()
    ctx = lax.axis_index("ctx")
    at = lambda xx, zz: {"ctx": xx * NZ + zz}
    z_peer = [None] + [at(x, turn(z + k, NZ)) for k in range(1, NZ)]
    x_peer = [None] + [at(turn(x + k, NX), z) for k in range(1, NX)]
    row_peer = [
        {"tr": turn(c + a, 2), "tc": turn(y + b, 4)} for a in range(2) for b in range(4) if (a, b) != (0, 0)
    ]
    x_right, x_far, x_left = x_peer[1:]
    z_right, z_left = z_peer[1], z_peer[7]
    sibling = {"tr": 1 - c}
    after, before = {"ctx": turn(ctx + 1, NX * NZ)}, {"ctx": turn(ctx + NX * NZ - 1, NX * NZ)}

    z_cross = [{**z_right, "tr": 1 - c}, {**z_left, "tr": 1 - c}]
    greeted = greet(z_peer[1:] + x_peer[1:] + row_peer + [after, before] + z_cross)

    def columns_of(group, j):
        start = WIDE if j == 0 else (j - 1) * COLS
        return pl.ds(pl.multiple_of(group * GROUP + start, 128), COLS)

    def slab(index):
        return pl.ds(pl.multiple_of(index * SLAB, 128), SLAB)

    def block(j, slot, piece=None):
        ref = wg0 if j == 0 else wg.at[j - 1]
        return ref.at[slot] if piece is None else ref.at[slot, piece]

    own_cols = pl.ds(pl.multiple_of(c * WIDE, 128), WIDE)
    sib_cols = pl.ds(pl.multiple_of((1 - c) * WIDE, 128), WIDE)

    small = []
    for k, (src, dst) in enumerate(
        (
            (w_step_hbm, w_step), (turns_hbm, turns), (ids_hbm, ids), (conv_w_hbm, conv_w), (conv_b_hbm, conv_b),
            (dt_bias_hbm, dt_bias), (rate_hbm, rate), (keep_hbm, keep), (skip_hbm, skip_row),
        )
    ):
        small.append(pltpu.make_async_copy(src, dst, s_small.at[k]))
        small[-1].start()
    local = []
    for j in range(CHUNKS):
        target = wg0.at[z, c, pl.ds(0, 64)] if j == 0 else wg.at[j - 1, z, c]
        copy = pltpu.make_async_copy(w_in.at[:, columns_of(c, j)], target, s_local.at[j])
        copy.start()
        local.append(copy)
    own_tokens = pltpu.make_async_copy(tokens.at[:, slab(x)], toks.at[0], s_own.at[0])
    own_tokens.start()
    own_gate = pltpu.make_async_copy(gate.at[:, own_cols], gates.at[c], s_own.at[1])
    own_gate.start()

    small[0].wait()
    small[1].wait()
    weights = w_step[...].astype(F32)
    blank = jnp.zeros((2 * HEAD_GROUP, 64), F32)
    weights = jnp.where(
        c == 0, jnp.concatenate([weights, blank], axis=1), jnp.concatenate([blank, weights], axis=1)
    )
    for group in range(2):
        rows = weights[group * HEAD_GROUP : (group + 1) * HEAD_GROUP].astype(BF16)
        step_rows[group] = jnp.concatenate([rows, jnp.zeros((HEAD_GROUP, 128), BF16)], axis=1)
    wg0[z, c, 64:80, :] = step_rows[c]
    flags[c] = jnp.broadcast_to(turns[...].astype(F32), (8, SPAN))

    pl.semaphore_wait(pltpu.get_barrier_semaphore(), greeted)

    started = []

    def send(src, dst, sems, index, device):
        if index is None:
            copy = remote(src, dst, sems[0], sems[1], device)
        else:
            copy = remote(src, dst, sems[0].at[index], sems[1].at[index], device)
        copy.start()
        started.append(copy)
        return copy

    def send_all(pieces, whole, sems):
        for src, dst, device in pieces:
            remote(src, dst, sems[0], sems[1], device).start()
        copy = remote(whole[0], whole[1], sems[0], sems[1], pieces[0][2])
        started.append(copy)
        return copy

    sib = (s_sib_s, s_sib_r)
    from_sibling = [
        [
            send(w_in.at[:, columns_of(1 - c, 0)], wg0.at[z, c, pl.ds(0, 64)], sib, 0, sibling),
            send(step_rows.at[1 - c], wg0.at[z, c, pl.ds(64, 16)], sib, 5, sibling),
        ]
    ]
    for j in (2, 1, 3, 4):
        from_sibling.append([send(w_in.at[:, columns_of(1 - c, j)], wg.at[j - 1, z, c], sib, j, sibling)])
    from_sibling = [from_sibling[0], from_sibling[2], from_sibling[1], from_sibling[3], from_sibling[4]]
    half = pl.multiple_of(c * 128, 128)
    tok = (s_tok_s, s_tok_r)
    far_slab, right_slab, left_slab = (slab(turn(x + k, NX)) for k in (2, 1, 3))
    relay_hop = [
        send(tokens.at[pl.ds(half + 64 * way, 64), far_slab], tok_relay.at[way], tok, way, device)
        for way, device in ((0, x_right), (1, x_left))
    ]
    near_hop = [
        send(tokens.at[pl.ds(half, 128), right_slab], toks.at[3, pl.ds(half, 128)], tok, 2, x_right),
        send(tokens.at[pl.ds(half, 128), left_slab], toks.at[1, pl.ds(half, 128)], tok, 3, x_left),
    ]
    hops = {}

    def ring_hop(h, j):
        sems = (s_ring_s, s_ring_r)
        if h == 0:
            local[j].wait()
        for way, sign, device in ((0, -1, z_right), (1, 1, z_left)):
            if h == 0:
                other = z_cross[way]
                target = wg0.at[z, c, pl.ds(0, 64)] if j == 0 else wg.at[j - 1, z, c]
                hops["r", way, 0, j] = send(block(j, z, c), block(j, z, c), sems, (way, 0, j), device)
                hops["rx", way, j] = [send(w_in.at[:, columns_of(1 - c, j)], target, sems, (way, 4, j), other)]
                if j == 0:
                    hops["rx", way, j].append(
                        send(step_rows.at[1 - c], wg0.at[z, c, pl.ds(64, 16)], sems, (way, 5, j), other)
                    )
                continue
            hops["r", way, h - 1, j].wait_recv()
            if h == 1:
                for copy in hops["rx", way, j]:
                    copy.wait_recv()
            slot = turn(z + sign * h + NZ, NZ)
            piece = None if h < 3 else way
            ref = block(j, slot, piece)
            hops["r", way, h, j] = send(ref, ref, sems, (way, h, j), device)

    def drain(keep):
        while len(started) > keep:
            started.pop(0).wait_send()

    row_at = lax.broadcasted_iota(jnp.int32, (SPAN, SPAN), 0)
    lane_at = lax.broadcasted_iota(jnp.int32, (SPAN, SPAN), 1)
    low_lanes = lane_at < HEAD_DIM
    id_rows = []

    def do_flags(_):
        hops["flag"] = send(flags.at[c], flags.at[c], (s_flag_s, s_flag_r), None, sibling)
        hops["gate"] = send(gate.at[:, sib_cols], gates.at[c], (s_gate_s, s_gate_r), None, sibling)
        for copy in small[2:]:
            copy.wait()
        prior = ids[pl.ds(jnp.maximum(2 * ctx - 1, 0), 1), :].astype(F32)
        id_rows.append(jnp.where(ctx == 0, -1.0, prior))
        for b in range(2):
            id_rows.append(ids[pl.ds(2 * ctx + b, 1), :].astype(F32))
        for b in range(3):
            id_col[b * SPAN : (b + 1) * SPAN] = jnp.broadcast_to(id_rows[b], (SPAN, SPAN)).T
        for k in range(3):
            masks[k] = (id_col[SPAN - 3 + k : SPAN - 3 + k + ROWS] == id_col[SPAN:]).astype(F32)
        rows = [jnp.concatenate([v[...], jnp.zeros((1, 96), F32)], axis=1) for v in (dt_bias, rate, keep, skip_row)]
        par[...] = jnp.concatenate(rows + [jnp.zeros((4, 128), F32)], axis=0)
        spread_row = lax.broadcasted_iota(jnp.int32, (SPAN, WIDE), 0)
        spread_lane = lax.shift_right_logical(lax.broadcasted_iota(jnp.int32, (SPAN, WIDE), 1), 6)
        spread[...] = (spread_lane == spread_row - 32).astype(F32)
        pick = (spread_lane == spread_row - c * HEAD_GROUP).astype(F32)
        wide_row[2] = jnp.dot(par[...], pick, precision=EXACT, preferred_element_type=F32)
        head_col[...] = jnp.concatenate([par[...], jnp.zeros((120, 128), F32)], axis=0).T

    def do_relay(_):
        for way, device in ((0, x_right), (1, x_left)):
            relay_hop[way].wait_recv()
            rows = pl.ds(half + 64 * way, 64)
            hops["relay", way] = send(tok_relay.at[way], toks.at[2, rows], tok, 4 + way, device)

    def share(d, way=None):
        rows = pl.ds(half, 128) if way is None else pl.ds(half + 64 * way, 64)
        ref, index = toks.at[d, rows], d - 1 if way is None else 3 * way + 1
        hops["share", index] = send(ref, ref, (s_fwd_s, s_fwd_r), index, sibling)

    def do_near(_):
        near_hop[0].wait_recv()
        share(3)
        near_hop[1].wait_recv()
        share(1)

    def do_far(_):
        for way in range(2):
            hops["relay", way].wait_recv()
            share(2, way)

    def do_toks(_):
        own_tokens.wait()
        for index in (0, 1, 2, 4):
            hops["share", index].wait_recv()

    def do_mul(j):
        for way in range(2):
            hops["r", way, 3, j].wait_recv()
        for copy in from_sibling[j]:
            copy.wait_recv()
        w = (wg0[:, :, :64, :] if j == 0 else wg[j - 1]).reshape(SLAB, COLS)
        far = jnp.dot(toks[2], w, preferred_element_type=F32)
        rel_out[j, 0] = far[:128].astype(BF16)
        rel_out[j, 1] = far[128:].astype(BF16)
        for way, device in ((0, x_right), (1, x_left)):
            hops["rel", way, j] = send(rel_out.at[j, way], rel_in.at[j, way], (s_rel_s, s_rel_r), (way, j), device)
        part[j, 1] = jnp.dot(toks[1], w, preferred_element_type=F32)
        part[j, 2] = jnp.dot(toks[3], w, preferred_element_type=F32)
        part[j, 0] = jnp.dot(toks[0], w, preferred_element_type=F32)

    def do_steps(_):
        heads = jnp.concatenate(
            [wg0[k, 0, 64:80, :128] + wg0[k, 1, 64:80, :128] for k in range(NZ)], axis=1
        )
        for d in (2, 1, 3, 0):
            sums = lax.dot_general(heads, toks[d], (((1,), (1,)), ((), ())), preferred_element_type=F32)
            if d == 0:
                dt_own[...] = sums
            else:
                dt_out[d - 1] = sums
                hops["dt", d] = send(dt_out.at[d - 1], dt_in.at[d - 1], (s_dt_s, s_dt_r), d - 1, x_peer[d])

    body = ROWS - RIM

    def send_sums(j, way, device):
        sems = (s_nb_s, s_nb_r)
        if j < LAST:
            hops["nb", way, j] = send(nb_out.at[j, way], nb_in.at[j, way], sems, (way, j), device)
            return
        rows = pl.ds(0, body)
        hops["nb", way, j] = send(nb_out.at[j, way, rows], nb_in.at[j, way, rows], sems, (way, j), device)

    def send_edge(way, device):
        rows = pl.ds(body, RIM)
        hops["edge", way] = send(
            nb_out.at[LAST, way, rows], nb_in.at[LAST, way, rows], (s_nb_s, s_nb_r), (way, CHUNKS), device
        )

    def do_pass(j):
        nb_out[j, 0, 128:] = part[j, 1, 128:].astype(BF16)
        nb_out[j, 1, :128] = part[j, 2, :128].astype(BF16)
        if j == LAST:
            send_edge(0, x_right)
        hops["rel", 0, j].wait_recv()
        nb_out[j, 0, :128] = (part[j, 1, :128] + rel_in[j, 0].astype(F32)).astype(BF16)
        if j < LAST:
            send_sums(j, 0, x_right)
        hops["rel", 1, j].wait_recv()
        nb_out[j, 1, 128:] = (part[j, 2, 128:] + rel_in[j, 1].astype(F32)).astype(BF16)
        if j == LAST:
            send_edge(1, x_left)
            send_sums(j, 0, x_right)
        send_sums(j, 1, x_left)

    def add_up(j, rows):
        return (part[j, 0, rows] + (nb_in[j, 0, rows].astype(F32) + nb_in[j, 1, rows].astype(F32))).astype(BF16)

    def send_rim(j):
        hops["rim", j] = send(
            xbc.at[j, pl.ds(ROWS, RIM)], xbc.at[j, pl.ds(0, RIM)], (s_rim_s, s_rim_r), j, after
        )

    def do_edge(_):
        hops["edge", 0].wait_recv()
        hops["edge", 1].wait_recv()
        xbc[LAST, ROWS:] = add_up(LAST, slice(body, ROWS))
        send_rim(LAST)

    def do_fin(j):
        hops["nb", 0, j].wait_recv()
        hops["nb", 1, j].wait_recv()
        if j == LAST:
            xbc[j, RIM:ROWS] = add_up(j, slice(0, body))
        else:
            xbc[j, RIM:] = add_up(j, slice(0, ROWS))
            send_rim(j)

    cums, steps, entered, left = [], [], [], []

    def do_dt(_):
        for d in (1, 2, 3):
            hops["dt", d].wait_recv()
        hops["flag"].wait_recv()
        mine = head_col[pl.ds(pl.multiple_of(c * HEAD_GROUP, 8), HEAD_GROUP), :]
        step = jax.nn.softplus(dt_own[...] + dt_in[0] + dt_in[1] + dt_in[2] + mine[:, 0:1])
        turned = jnp.concatenate([flags[0, 0:1, :], flags[1, 0:1, :]], axis=1)
        log_decay = -mine[:, 1:2] * step + turned * jnp.log(mine[:, 2:3])
        upper = (row_at <= lane_at).astype(F32)
        for b in range(2):
            span = slice(b * SPAN, (b + 1) * SPAN)
            row, before_it = id_rows[b + 1], id_rows[b][:, SPAN - 1 :]
            cum = jnp.dot(log_decay[:, span], upper, precision=EXACT, preferred_element_type=F32)
            steps.append(step[:, span])
            cums.append(cum)
            to_end = jnp.where(row == row[:, SPAN - 1 :], jnp.exp(cum[:, SPAN - 1 :] - cum) * step[:, span], 0.0)
            from_start = jnp.where(row == before_it, jnp.exp(cum), 0.0)
            columns[b] = jnp.concatenate([cum, to_end, from_start, jnp.zeros((80, SPAN), F32)], axis=0).T
            wide_row[b] = jnp.dot(columns[b, 120:128], spread[...], precision=EXACT, preferred_element_type=F32)
        d_out[...] = columns[0, 120:128] * columns[1, 120:128]
        d_in[z] = d_out[...]
        seven = d_in.at[pl.ds(0, 7)]
        hops["d"] = send_all([(d_out, d_in.at[z], z_peer[k]) for k in range(1, NZ)], (seven, seven), (s_d_s, s_d_r))

    def expand(b, first):
        return jnp.where(low_lanes, columns[b, :, first : first + 1], columns[b, :, first + 1 : first + 2])

    def conv(j, part_of):
        lanes = slice(part_of * 128, (part_of + 1) * 128)
        start = (WIDE if j == 0 else (j - 1) * COLS) + part_of * 128
        at_channels = pl.ds(pl.multiple_of(c * GROUP + start, 128), 128)
        ext = xbc[j, :, lanes].astype(F32)
        total = conv_b[pl.ds(c * (GROUP // 128) + start // 128, 1), :] + jnp.zeros((ROWS, 128), F32)
        for k in range(3):
            total = total + conv_w[k : k + 1, at_channels] * ext[RIM - 3 + k : RIM - 3 + k + ROWS] * masks[k]
        total = total + conv_w[3:4, at_channels] * ext[RIM:]
        return jax.nn.silu(total).astype(BF16)

    def do_bc(_):
        hops["rim", 0].wait_recv()
        b_matrix = conv(0, 0)
        bc[1] = conv(0, 1)
        bc[0] = b_matrix
        for b in range(2):
            bc[2, b * SPAN : (b + 1) * SPAN] = b_matrix[b * SPAN : (b + 1) * SPAN].T

    def do_st(j):
        hops["rim", j].wait_recv()
        q = j - 1
        for pair in range(2):
            lanes = slice(pair * 128, (pair + 1) * 128)
            heads = conv(j, pair)
            xs[q, :, lanes] = heads
            for b in range(2):
                span = slice(b * SPAN, (b + 1) * SPAN)
                scaled = (heads[span].astype(F32) * expand(b, 16 + 4 * q + 2 * pair)).astype(BF16)
                states[q, b, :, lanes] = jnp.dot(bc[2, span], scaled, preferred_element_type=F32)
        decay = wide_row[1, 7:8, q * COLS : (q + 1) * COLS]
        state_bf[q] = (decay * states[q, 0] + states[q, 1]).astype(BF16).reshape(NZ, 16, COLS)
        st_in[q, z] = state_bf[q, z]
        hops["st", q] = send_all(
            [(state_bf.at[q, turn(z + k, NZ)], st_in.at[q, z], z_peer[k]) for k in (4, 3, 5, 2, 6, 1, 7)],
            (state_bf.at[q, pl.ds(0, 7)], st_in.at[q, pl.ds(0, 7)]),
            (s_st_s.at[q], s_st_r.at[q]),
        )

    def do_diag(j):
        q = j - 1
        for b in range(2):
            span = slice(b * SPAN, (b + 1) * SPAN)
            scores = lax.dot_general(
                bc[1, span], bc[0, span], (((1,), (1,)), ((), ())), preferred_element_type=F32
            )
            allowed = (id_col[SPAN + b * SPAN : 2 * SPAN + b * SPAN] == id_rows[b + 1]) & (row_at >= lane_at)
            for pair in range(2):
                lanes = slice(pair * 128, (pair + 1) * 128)
                halves = []
                for h in (4 * q + 2 * pair, 4 * q + 2 * pair + 1):
                    gap = jnp.where(allowed, columns[b, :, h : h + 1] - cums[b][h : h + 1], -jnp.inf)
                    halves.append((scores * jnp.exp(gap) * steps[b][h : h + 1]).astype(BF16))
                heads = xs[q, span, lanes]
                zero = jnp.zeros_like(heads)
                both = jnp.concatenate([jnp.where(low_lanes, heads, zero), jnp.where(low_lanes, zero, heads)], axis=0)
                diag = jnp.dot(jnp.concatenate(halves, axis=1), both, preferred_element_type=F32)
                skip = wide_row[2, 3:4, q * COLS + pair * 128 : q * COLS + (pair + 1) * 128]
                osum[q, span, lanes] = diag + skip * heads.astype(F32)

    def do_zs(j):
        q = j - 1
        if "e" not in hops:
            hops["d"].wait_recv()
            per_chip = jnp.concatenate([d_in[k, 7:8] for k in range(NZ)], axis=0)
            wide_z[...] = jnp.dot(per_chip, spread[...], precision=EXACT, preferred_element_type=F32)
            row_decay = per_chip[0:1]
            for k in range(1, NZ):
                row_decay = row_decay * per_chip[k : k + 1]
            e_out[...] = jnp.broadcast_to(row_decay, (8, 128))
            e_in[x] = e_out[...]
            three = e_in.at[pl.ds(0, 3)]
            hops["e"] = send_all([(e_out, e_in.at[x], x_peer[k]) for k in (2, 1, 3)], (three, three), (s_e_s, s_e_r))
        hops["st", q].wait_recv()
        running = jnp.zeros((16, COLS), F32)
        for k in range(NZ):
            pre[q, k] = running
            running = wide_z[k : k + 1, q * COLS : (q + 1) * COLS] * running + st_in[q, k].astype(F32)
        tot_out[q] = running.astype(BF16)
        tot_in[q, x] = tot_out[q]
        three = tot_in.at[q, pl.ds(0, 3)]
        hops["t", q] = send_all(
            [(tot_out.at[q], tot_in.at[q, x], x_peer[k]) for k in (2, 1, 3)], (three, three), (s_t_s.at[q], s_t_r.at[q])
        )

    def do_xs(j):
        q = j - 1
        lanes = slice(q * COLS, (q + 1) * COLS)
        if not entered:
            entered.append(j)
            hops["e"].wait_recv()
            wide_x[...] = jnp.dot(
                jnp.concatenate([e_in[k] for k in range(NX)], axis=0), spread[...], precision=EXACT,
                preferred_element_type=F32,
            )
        hops["t", q].wait_recv()
        entering = jnp.zeros((16, COLS), F32)
        for k in range(NX):
            entering = jnp.where(
                k < x, wide_x[8 * k : 8 * k + 1, lanes] * entering + tot_in[q, k].astype(F32), entering
            )
        for k in range(NZ):
            back_out[q, k] = (pre[q, k] + entering).astype(BF16)
            entering = entering * wide_z[k : k + 1, lanes]
        back_in[q, z] = back_out[q, z]
        hops["b", q] = send_all(
            [(back_out.at[q, turn(z + k, NZ)], back_in.at[q, z], z_peer[k]) for k in (4, 3, 5, 2, 6, 1, 7)],
            (back_out.at[q, pl.ds(0, 7)], back_in.at[q, pl.ds(0, 7)]),
            (s_b_s.at[q], s_b_r.at[q]),
        )

    def do_out(j):
        q = j - 1
        first = not left
        left.append(j)
        if first:
            own_gate.wait()
            hops["gate"].wait_recv()
        hops["b", q].wait_recv()
        for pair in range(2):
            lanes = slice(pair * 128, (pair + 1) * 128)
            cols = slice(q * COLS + pair * 128, q * COLS + (pair + 1) * 128)
            carried = back_in[q, :, :, lanes].reshape(STATE, 128)
            later = (wide_row[0, 7:8, cols] * carried.astype(F32) + states[q, 0, :, lanes]).astype(BF16)
            for b, state in ((0, carried), (1, later)):
                span = slice(b * SPAN, (b + 1) * SPAN)
                off = jnp.dot(bc[1, span], state, preferred_element_type=F32) * expand(b, 32 + 4 * q + 2 * pair)
                rows = (osum[q, span, lanes] + off) * jax.nn.silu(gates[b, :, cols].astype(F32))
                gated[q, b, :, lanes] = rows
                squares[b] = rows * rows if first and pair == 0 else squares[b] + rows * rows
        hops["g", q] = send(gated.at[q, 1 - c], gated_sib.at[q], (s_g_s, s_g_r), q, sibling)

    act = {
        "flags": do_flags, "relay": do_relay, "near": do_near, "far": do_far, "toks": do_toks, "mul": do_mul, "steps": do_steps, "pass": do_pass,
        "fin": do_fin, "edge": do_edge, "dt": do_dt, "bc": do_bc, "st": do_st, "diag": do_diag, "drain": lambda _: drain(14), "zs": do_zs, "xs": do_xs, "out": do_out,
    }
    for word in ORDER:
        if word[0] == "r" and word[1:].isdigit():
            ring_hop(int(word[1]), int(word[2]))
        elif word[-1].isdigit():
            act[word[:-1]](int(word[-1]))
        else:
            act[word](0)

    sums = [jnp.sum(squares[b].T, axis=0, keepdims=True) for b in range(2)]
    sq_out[...] = jnp.concatenate(sums + [jnp.zeros((6, SPAN), F32)], axis=0)
    send_all(
        [(sq_out, sq_in.at[k], device) for k, device in enumerate(row_peer)], (sq_in, sq_in), (s_q_s, s_q_r)
    ).wait_recv()
    total = sq_out[...]
    for k in range(7):
        total = total + sq_in[k]
    scale = lax.rsqrt(total / INNER + EPSILON)
    scale = jnp.where(c == 0, scale[0:1], scale[1:2])
    scale = jnp.broadcast_to(scale, (SPAN, SPAN)).T
    for q in range(4):
        hops["g", q].wait_recv()
        for pair in range(2):
            lanes = slice(pair * 128, (pair + 1) * 128)
            for group, rows in ((c, gated[q, c, :, lanes]), (1 - c, gated_sib[q, :, lanes])):
                cols = pl.ds(pl.multiple_of(group * WIDE + q * COLS + pair * 128, 128), 128)
                out[:, cols] = rows * scale
    drain(0)


def layer(*arrays):
    sem = pltpu.SemaphoreType.DMA
    vmem, hbm = pl.BlockSpec(memory_space=pltpu.VMEM), pl.BlockSpec(memory_space=pltpu.HBM)

    def pair(*shape):
        return [sem(shape)] * 2 if shape else [sem] * 2

    return pl.pallas_call(
        layer_kernel,
        out_shape=jax.ShapeDtypeStruct((SPAN, 2 * WIDE), F32),
        in_specs=[hbm] * 12,
        out_specs=vmem,
        scratch_shapes=[
            pltpu.VMEM((2 * HEAD_GROUP, 64), BF16),
            pltpu.VMEM((4, 2 * GROUP), F32),
            pltpu.VMEM((2 * GROUP // 128, 128), F32),
            pltpu.VMEM((1, 2 * HEAD_GROUP), F32),
            pltpu.VMEM((1, 2 * HEAD_GROUP), F32),
            pltpu.VMEM((1, 2 * HEAD_GROUP), F32),
            pltpu.VMEM((1, 2 * HEAD_GROUP), F32),
            pltpu.VMEM((8, 128), F32),
            pltpu.VMEM((64, SPAN), jnp.int32),
            pltpu.VMEM((1, SPAN), jnp.int32),
            pltpu.VMEM((NX, ROWS, SLAB), BF16),
            pltpu.VMEM((2, 64, SLAB), BF16),
            pltpu.VMEM((NZ, 2, 80, COLS), BF16),
            pltpu.VMEM((CHUNKS - 1, NZ, 2, 64, COLS), BF16),
            pltpu.VMEM((2, HEAD_GROUP, COLS), BF16),
            pltpu.VMEM((CHUNKS, 3, ROWS, COLS), F32),
            pltpu.VMEM((CHUNKS, 2, 128, COLS), BF16),
            pltpu.VMEM((CHUNKS, 2, 128, COLS), BF16),
            pltpu.VMEM((CHUNKS, 2, ROWS, COLS), BF16),
            pltpu.VMEM((CHUNKS, 2, ROWS, COLS), BF16),
            pltpu.VMEM((3, HEAD_GROUP, ROWS), F32),
            pltpu.VMEM((3, HEAD_GROUP, ROWS), F32),
            pltpu.VMEM((HEAD_GROUP, ROWS), F32),
            pltpu.VMEM((2, 8, SPAN), F32),
            pltpu.VMEM((CHUNKS, RIM + ROWS, COLS), BF16),
            pltpu.VMEM((3 * SPAN, SPAN), F32),
            pltpu.VMEM((3, ROWS, 128), F32),
            pltpu.VMEM((SPAN, WIDE), F32),
            pltpu.VMEM((128, 128), F32),
            pltpu.VMEM((2, SPAN, 128), F32),
            pltpu.VMEM((3, 8, WIDE), F32),
            pltpu.VMEM((3, ROWS, STATE), BF16),
            pltpu.VMEM((4, ROWS, COLS), BF16),
            pltpu.VMEM((4, ROWS, COLS), F32),
            pltpu.VMEM((4, 2, STATE, COLS), F32),
            pltpu.VMEM((4, NZ, 16, COLS), BF16),
            pltpu.VMEM((4, NZ, 16, COLS), BF16),
            pltpu.VMEM((8, 128), F32),
            pltpu.VMEM((NZ, 8, 128), F32),
            pltpu.VMEM((NZ, WIDE), F32),
            pltpu.VMEM((4, NZ, 16, COLS), F32),
            pltpu.VMEM((4, 16, COLS), BF16),
            pltpu.VMEM((4, NX, 16, COLS), BF16),
            pltpu.VMEM((8, 128), F32),
            pltpu.VMEM((NX, 8, 128), F32),
            pltpu.VMEM((8 * NX, WIDE), F32),
            pltpu.VMEM((4, NZ, 16, COLS), BF16),
            pltpu.VMEM((4, NZ, 16, COLS), BF16),
            pltpu.VMEM((2, SPAN, WIDE), BF16),
            pltpu.VMEM((4, 2, SPAN, COLS), F32),
            pltpu.VMEM((4, SPAN, COLS), F32),
            pltpu.VMEM((2, SPAN, 128), F32),
            pltpu.VMEM((8, 128), F32),
            pltpu.VMEM((7, 8, 128), F32),
            sem((9,)),
            sem((CHUNKS,)),
            sem((2,)),
            *pair(CHUNKS + 1),
            *pair(2, 6, CHUNKS),
            *pair(6),
            *pair(5),
            *pair(2, CHUNKS),
            *pair(2, CHUNKS + 1),
            *pair(3),
            *pair(CHUNKS),
            *pair(),
            *pair(),
            *pair(4),
            *pair(),
            *pair(4),
            *pair(),
            *pair(4),
            *pair(),
            *pair(4),
        ],
        compiler_params=pltpu.CompilerParams(
            collective_id=0, has_side_effects=True, vmem_limit_bytes=62 * 2**20
        ),
    )(*arrays)


def shards(
    tokens, w_in, w_step, conv_weight, conv_bias, dt_bias, decay_rate, turn_keep, skip, norm_gain, gate,
    segment_ids, turn_start,
):
    rows = layer(
        tokens, w_in, w_step.T, conv_weight, conv_bias.reshape(-1, 128), dt_bias[None], decay_rate[None],
        turn_keep[None], skip[None], gate, segment_ids.reshape(-1, SPAN), turn_start[None],
    )
    return (rows * norm_gain[None, :]).astype(BF16)


def solution(mesh):
    in_specs = (
        P("ctx", None),
        P(("ctx", "tr"), "tc"),
        P(("ctx", "tr"), "tc"),
        P(None, "tc"),
        P("tc"),
        P("tc"),
        P("tc"),
        P("tc"),
        P("tc"),
        P("tc"),
        P(("ctx", "tr"), "tc"),
        P(),
        P(("ctx", "tr")),
    )
    out_specs = P(("ctx", "tr"), "tc")
    return jax.shard_map(shards, mesh=mesh, in_specs=in_specs, out_specs=out_specs, check_vma=False)
```
